512 devices in a mesh: pair: 64 (over y, z), ints: 8 (over x, core).
Axes of the slice: x: 4, y: 4, z: 16, core: 2. Of those that a mesh axis runs over, the one named last changes fastest.
Arguments:
- amp_tiles: bfloat16 [1536, 128, 128], P('pair'), may hold values from -6 to 6
- amp_row: int32 [64, 24], replicated, may hold values from 0 to 1
- amp_col: int32 [64, 24], replicated, may hold values from 0 to 23
- amp_dest: int32 [64, 24], replicated, may hold values from 0 to 127, as said below
- amp_count: int32 [64], replicated, may hold values from 12 to 24, as said below
- ladder_ints: bfloat16 [3072, 3072], P('pair', 'ints'), may hold values from -0.21875 to 0.21875
- ladder_present: int32 [24, 24], P(None, 'ints'), may hold values 0 or 1
- cycle_ints: bfloat16 [3072, 3072], P('pair', 'ints'), may hold values from -0.21875 to 0.21875
- cycle_present: int32 [24, 24], P(None, 'ints'), may hold values 0 or 1
Outputs:
- ladder: bfloat16 [16384, 3072], P('pair', 'ints')
- cycle: bfloat16 [16384, 3072], P('pair', 'ints')
The draws below stay inside these ranges and needn't reach their ends.
Inputs may be any that keep to these rules, and one draw needn't show every extreme that they name: On each pair device, amp_dest // 2 names every pair device at most 2 times over the 24 slots, and some device exactly 2 times. `amp_count`: some pair device uses all 24 slots.
All inputs are finite; a program needn't handle non-finite values. No bound on the sum of `ladder_present` or of `cycle_present` on one device may be relied on, other than what follows from the above.
Results may differ from the reference program's by a relative error of at most 0.0041.
Values may be sent and summed in bfloat16 or wider, within the bound.
A program may use at most 64 MiB of HBM per device.

```python
import jax
import jax.numpy as jnp
from jax import lax

TILE = 128
RT_DEV = 2
NCT = 24
NROW = 128
SLOTS = 24
CAP = 2
N_PAIR = 64


def draw_amp_dest(key, part):
    key = jax.random.fold_in(key, 11)
    first, second, third, fourth = jax.random.split(key, 4)
    hot = jax.random.permutation(first, N_PAIR) < max(1, N_PAIR // 8)
    weight = jnp.where(hot, 4, 1).astype(jnp.int32)
    score = jax.random.randint(second, (N_PAIR, N_PAIR), 0, 4096) * weight[None, :]
    score = score * N_PAIR + jnp.arange(N_PAIR)[None, :]
    order = jnp.argsort(-score, axis=1, stable=True)
    chosen = order[:, :SLOTS // CAP]
    devices = jnp.repeat(chosen, CAP, axis=1)
    shuffle = jax.random.randint(third, (N_PAIR, SLOTS), 0, 65536) * SLOTS + jnp.arange(SLOTS)[None, :]
    devices = jnp.take_along_axis(devices, jnp.argsort(shuffle, axis=1, stable=True), axis=1)
    rows = jax.random.randint(fourth, (N_PAIR, SLOTS), 0, RT_DEV)
    return (devices * RT_DEV + rows).astype(jnp.int32)


def draw_amp_count(key, part):
    key = jax.random.fold_in(key, 23)
    first, second = jax.random.split(key)
    counts = jax.random.randint(first, (N_PAIR,), SLOTS // 2, SLOTS + 1)
    where = jax.random.randint(second, (), 0, N_PAIR)
    return counts.at[where].set(SLOTS).astype(jnp.int32)


def place_ends(array, own_key, smallest, top_value):
    extent = array.shape
    spot = [jax.random.randint(jax.random.fold_in(own_key, axis), (), 0, extent[axis]) for axis in range(len(extent))]
    array = array.at[tuple(spot)].set(smallest)
    longest = extent.index(max(extent))
    spot[longest] = (spot[longest] + 1) % extent[longest]
    return array.at[tuple(spot)].set(top_value)


def level_of(own_key, dims, cuts, low, high):
    factor_of = 1.0
    for dim, parts in cuts:
        heights = jax.random.uniform(jax.random.fold_in(jax.random.fold_in(own_key, 6), dim), (parts,), jnp.float32, low / len(cuts), high / len(cuts))
        factor_of = factor_of * jnp.repeat(jnp.exp(heights), dims[dim] // parts).reshape((-1,) + (1,) * (len(dims) - 1 - dim))
    return factor_of


def bell_draw(key, extent, width, most, shards=(), dtype=jnp.bfloat16):
    values = jax.random.normal(key, extent, jnp.float32) * width
    if len(shards) > 0:
        values = level_of(key, extent, shards, -0.22, 0.18) * values
    return jnp.clip(values, min=-most, max=most).astype(dtype)


def setup_inputs(seed: int = 0) -> dict:
    seeds = jax.random.split(jax.random.key(seed), 10)
    return {
        "amp_tiles": bell_draw(seeds[0], (N_PAIR * SLOTS, TILE, TILE), 1.0, 6.0, ((0, 64),)),
        "amp_row": place_ends(jax.random.randint(seeds[1], (N_PAIR, SLOTS), 0, RT_DEV), jax.random.fold_in(seeds[1], 1), 0, RT_DEV - 1).astype(jnp.int32),
        "amp_col": place_ends(jax.random.randint(seeds[2], (N_PAIR, SLOTS), 0, NCT), jax.random.fold_in(seeds[2], 1), 0, NCT - 1).astype(jnp.int32),
        "amp_dest": draw_amp_dest(jax.random.fold_in(seeds[9], 71), 0),
        "amp_count": draw_amp_count(jax.random.fold_in(seeds[9], 71), 0),
        "ladder_ints": bell_draw(seeds[5], (NCT * TILE, NCT * TILE), (SLOTS * TILE // (2 * RT_DEV)) ** -0.5, 0.21875, ((0, 64), (1, 8))),
        "ladder_present": place_ends((jax.random.randint(seeds[6], (NCT, NCT), 0, 2) < 1).astype(jnp.int32), jax.random.fold_in(seeds[6], 1), 0, 1),
        "cycle_ints": bell_draw(seeds[7], (NCT * TILE, NCT * TILE), (SLOTS * TILE // (2 * RT_DEV)) ** -0.5, 0.21875, ((0, 64), (1, 8))),
        "cycle_present": place_ends((jax.random.randint(seeds[8], (NCT, NCT), 0, 2) < 1).astype(jnp.int32), jax.random.fold_in(seeds[8], 1), 0, 1),
    }


def assemble(tiles, index, weight):
    grid = jnp.zeros((RT_DEV * NCT, TILE, TILE), jnp.float32)
    grid = grid.at[index].add(tiles.astype(jnp.float32) * weight[:, None, None])
    grid = grid.reshape(RT_DEV, NCT, TILE, TILE).transpose(0, 2, 1, 3)
    return grid.reshape(RT_DEV * TILE, NCT * TILE).astype(jnp.bfloat16)


def expand(present):
    return jnp.repeat(jnp.repeat(present, TILE, axis=0), TILE, axis=1).astype(jnp.bfloat16)


def reference(amp_tiles, amp_row, amp_col, amp_dest, amp_count, ladder_ints, ladder_present, cycle_ints, cycle_present):
    active = (jnp.arange(SLOTS)[None, :] < amp_count[:, None]).astype(jnp.float32)
    tiles = amp_tiles.reshape(N_PAIR, SLOTS, TILE, TILE)
    ladder_w = ladder_ints * expand(ladder_present)
    cycle_w = cycle_ints * expand(cycle_present)

    def ladder_one(source):
        index = (amp_row[source] * NCT + amp_col[source]).astype(jnp.int32)
        grid = assemble(tiles[source], index, active[source])
        return jnp.dot(grid, ladder_w, preferred_element_type=jnp.float32).astype(jnp.bfloat16)

    ladder = lax.map(ladder_one, jnp.arange(N_PAIR)).reshape(NROW * TILE, NCT * TILE)
    flipped = jnp.swapaxes(amp_tiles, 1, 2)
    cycle_index = ((amp_dest % RT_DEV) * NCT + amp_col).reshape(-1).astype(jnp.int32)
    owner = (amp_dest // RT_DEV).reshape(-1)
    flat_active = active.reshape(-1)

    def cycle_one(target):
        weight = flat_active * (owner == target).astype(jnp.float32)
        grid = assemble(flipped, cycle_index, weight)
        return jnp.dot(grid, cycle_w, preferred_element_type=jnp.float32).astype(jnp.bfloat16)

    cycle = lax.map(cycle_one, jnp.arange(N_PAIR)).reshape(NROW * TILE, NCT * TILE)
    return ladder, cycle
```

```python
import jax
import jax.numpy as jnp
from jax import lax
from jax.experimental import pallas as pl
from jax.experimental.pallas import tpu as pltpu
from jax.sharding import PartitionSpec as P

TILE = 128
NCT = 24
SLOTS = 24
NY = 4
NZ = 16
NX = 4
PART = 16
ROWS = 48
COLS = 384
HALF = NZ // 2
MESH = pl.DeviceIdType.MESH
F32 = jnp.float32
BF16 = jnp.bfloat16


def kernel(
    lp, cp, sel, order, cont, last, some, a_order, a_cont, a_last, a_some,
    wl, wr, tiles,
    out_l, out_c,
    w, t, ysend, yrecv, pre, bt, a_src, a_pre, a, acc,
    loc, zw_s, zw_r, zt_s, zt_r, y1_s, y1_r, y2_s, y2_r, ya_s, ya_r, xs_s, xs_r, co_s, co_r,
):
    p = lax.axis_index("pair")
    i = lax.axis_index("ints")
    y, z = p // NZ, p % NZ
    x, core = i // 2, i % 2

    def at(yy, zz):
        return (lax.rem(yy + NY, NY) * NZ + lax.rem(zz + NZ, NZ), i)

    def at_x(xx):
        return (p, lax.rem(xx + NX, NX) * 2 + core)

    zn = (at(y, z + 1), at(y, z - 1))
    yn = (at(y + 1, z), at(y - 1, z))
    xn = (at_x(x + 1), at_x(x - 1))
    twin = (p, x * 2 + 1 - core)

    tile_here = pltpu.make_async_copy(
        tiles.at[:, pl.ds(pl.multiple_of(PART * i, PART), PART), :],
        t.at[pl.ds(z * SLOTS, SLOTS)], loc.at[0])
    tile_here.start()
    tile_all = pltpu.make_async_copy(tiles, a_src, loc.at[1])
    tile_all.start()

    barrier = pltpu.get_barrier_semaphore()
    greet = (*zn, *yn, at(y + 2, z), *xn, twin)
    for dev in greet:
        pl.semaphore_signal(barrier, inc=1, device_id=dev, device_id_type=MESH)

    for k, (src, present) in enumerate(((wl, lp), (wr, cp))):
        for g in range(ROWS // PART):
            row = (3 * p + g) // 8
            for n in range(COLS // TILE):
                keep = present[row * 3 + n].astype(F32)
                block = src[g * PART:(g + 1) * PART, n * TILE:(n + 1) * TILE].astype(F32)
                w[k, pl.ds(pl.multiple_of(ROWS * p + g * PART, PART), PART), n * TILE:(n + 1) * TILE] = (
                    block * keep).astype(BF16)
    tile_here.wait()
    pl.semaphore_wait(barrier, len(greet))

    sends = []

    def send(src, dst, ss, rs, dev):
        c = pltpu.make_async_remote_copy(
            src_ref=src, dst_ref=dst, send_sem=ss, recv_sem=rs, device_id=dev, device_id_type=MESH)
        c.start()
        sends.append(c)

    def arrived(buf, ss, rs, dev):
        pltpu.make_async_remote_copy(
            src_ref=buf, dst_ref=buf, send_sem=ss, recv_sem=rs, device_id=dev, device_id_type=MESH).wait_recv()

    def w_at(yy, zz, part=None):
        q = lax.rem(yy + NY, NY) * NZ + lax.rem(zz + NZ, NZ)
        rows = pl.ds(pl.multiple_of(q * ROWS, PART), ROWS)
        if part is None:
            return w.at[:, rows, :]
        return w.at[part, rows, :]

    def t_at(zz, part=None):
        q = lax.rem(zz + NZ, NZ)
        if part is None:
            return t.at[pl.ds(q * SLOTS, SLOTS)]
        return t.at[pl.ds(q * SLOTS + part * (SLOTS // 2), SLOTS // 2)]

    def y_forward(zz, j):
        for d in range(2):
            send(w_at(y, zz), w_at(y, zz), y1_s.at[d, j], y1_r.at[d, j], yn[d])

    def place_a(j, run):
        run = a_src[a_order[j]].astype(F32) + a_cont[j] * run
        a_pre[j] = run
        return run

    y_forward(z, 0)
    for s in range(HALF):
        for d in range(2):
            zz = z - s if d == 0 else z + s
            part = d if s == HALF - 1 else None
            send(w_at(y, zz, part), w_at(y, zz, part), zw_s.at[d, s], zw_r.at[d, s], zn[d])
            send(t_at(zz, part), t_at(zz, part), zt_s.at[d, s], zt_r.at[d, s], zn[d])
        if s == 0:
            tile_all.wait()
            lax.fori_loop(0, SLOTS, place_a, jnp.zeros((TILE, TILE), F32))
        if s in (1, 2):
            r = s - 1
            for c in range(NCT):
                a[r * TILE:(r + 1) * TILE, c * TILE:(c + 1) * TILE] = (
                    a_pre[a_last[r * NCT + c]] * a_some[r * NCT + c]).astype(BF16)
        for d in range(2):
            zz = z - s - 1 if d == 0 else z + s + 1
            part = d if s == HALF - 1 else None
            arrived(w_at(y, zz, part), zw_s.at[d, s], zw_r.at[d, s], zn[d])
            if s < HALF - 1:
                y_forward(zz, 2 * s + 1 + d)
        if s == HALF - 1:
            y_forward(z - HALF, NZ - 1)
        for d in range(2):
            zz = z - s - 1 if d == 0 else z + s + 1
            part = d if s == HALF - 1 else None
            arrived(t_at(zz, part), zt_s.at[d, s], zt_r.at[d, s], zn[d])

    for dy in (1, 2, 3, 0):
        first = lax.rem(y + dy, NY) * 32

        def choose(j, _, dy=dy, first=first):
            tile = t[sel[first + j]]
            if dy == 0:
                yrecv[y * 32 + j] = tile
            else:
                ysend[(dy - 1) * 32 + j] = tile
            return 0

        lax.fori_loop(0, 32, choose, 0, unroll=8)
        if dy > 0:
            send(ysend.at[pl.ds((dy - 1) * 32, 32)], yrecv.at[pl.ds(y * 32, 32)],
                 ya_s.at[dy - 1], ya_r.at[dy - 1], at(y + dy, z))

    def step_z(j):
        if j == 0:
            return z
        if j == NZ - 1:
            return z - HALF
        s = (j + 1) // 2
        return z - s if j % 2 == 1 else z + s

    for j in range(NZ):
        zz = step_z(j)
        for d in range(2):
            yy = y - 1 if d == 0 else y + 1
            arrived(w_at(yy, zz), y1_s.at[d, j], y1_r.at[d, j], yn[d])
            send(w_at(yy, zz, d), w_at(yy, zz, d), y2_s.at[d, j], y2_r.at[d, j], yn[d])

    for dy in (1, 2, 3):
        yy = lax.rem(y - dy + NY, NY)
        arrived(yrecv.at[pl.ds(yy * 32, 32)], ya_s.at[dy - 1], ya_r.at[dy - 1], at(y + dy, z))

    def add_up(j, run):
        run = yrecv[order[j]].astype(F32) + cont[j] * run
        pre[j] = run
        return run

    lax.fori_loop(0, 128, add_up, jnp.zeros((PART, TILE), F32), unroll=8)

    def bt_at(ii, lo=0, num=NCT):
        return bt.at[pl.ds(lo, num), pl.ds(pl.multiple_of(ii * PART, PART), PART), :]

    for q in range(2 * NCT):
        c, r = q // 2, q % 2
        bt[c, pl.ds(pl.multiple_of(i * PART, PART), PART), r * TILE:(r + 1) * TILE] = (
            pre[last[q]] * some[q]).astype(BF16)

    for d in range(2):
        send(bt_at(i), bt_at(i), xs_s.at[d], xs_r.at[d], xn[d])
    send(bt_at(i), bt_at(i), co_s.at[0], co_r.at[0], twin)
    half = NCT // 2
    for d in range(2):
        ii = xn[1 - d][1]
        arrived(bt_at(ii), xs_s.at[d], xs_r.at[d], xn[d])
        send(bt_at(ii, d * half, half), bt_at(ii, d * half, half), xs_s.at[2 + d], xs_r.at[2 + d], xn[d])
        send(bt_at(ii), bt_at(ii), co_s.at[1 + d], co_r.at[1 + d], twin)
    far = at_x(x + 2)[1]
    for d in range(2):
        arrived(bt_at(far, d * half, half), xs_s.at[2 + d], xs_r.at[2 + d], xn[d])
        send(bt_at(far, d * half, half), bt_at(far, d * half, half), co_s.at[3 + d], co_r.at[3 + d], twin)

    for j in range(NZ):
        zz = step_z(j)
        for d in range(2):
            arrived(w_at(y + 2, zz, d), y2_s.at[d, j], y2_r.at[d, j], yn[d])

    depth = 512
    acc[...] = jnp.zeros_like(acc)

    @pl.loop(0, NCT * TILE // depth)
    def _(k):
        cut = pl.ds(pl.multiple_of(k * depth, depth), depth)
        acc[...] += jnp.dot(a[:, cut], w[0, cut, :], preferred_element_type=F32)

    out_l[...] = acc[...].astype(BF16)

    def other(ii):
        return lax.div(ii, 2) * 2 + 1 - lax.rem(ii, 2)

    arrived(bt_at(other(i)), co_s.at[0], co_r.at[0], twin)
    for d in range(2):
        arrived(bt_at(other(xn[1 - d][1])), co_s.at[1 + d], co_r.at[1 + d], twin)
    for d in range(2):
        arrived(bt_at(other(far), d * half, half), co_s.at[3 + d], co_r.at[3 + d], twin)

    acc[...] = jnp.zeros_like(acc)

    @pl.loop(0, NCT * TILE // depth)
    def _(k):
        cut = pl.ds(pl.multiple_of(k * depth, depth), depth)
        part = bt[pl.ds(k * (depth // TILE), depth // TILE)].reshape(depth, 2 * TILE)
        acc[...] += lax.dot_general(
            part, w[1, cut, :], (((0,), (0,)), ((), ())), preferred_element_type=F32)

    out_c[...] = acc[...].astype(BF16)

    for c in sends:
        c.wait_send()


def chain(key, places):
    n = key.shape[0]
    ids = jnp.arange(n)
    before = (key[:, None] < key[None, :]) | ((key[:, None] == key[None, :]) & (ids[:, None] < ids[None, :]))
    rank = jnp.sum(before.astype(jnp.int32), axis=0)
    here = (rank[None, :] == ids[:, None]).astype(jnp.int32)
    order = jnp.sum(here * ids[None, :], axis=1)
    same = (key[:, None] == key[None, :]) & (ids[:, None] < ids[None, :])
    joined = (jnp.sum(same.astype(jnp.int32), axis=0) > 0).astype(jnp.int32)
    cont = jnp.sum(here * joined[None, :], axis=1).astype(F32)
    spots = jnp.arange(places)
    last = jnp.sum((key[None, :] <= spots[:, None]).astype(jnp.int32), axis=1) - 1
    some = jnp.any(key[None, :] == spots[:, None], axis=1).astype(F32)
    return order, cont, jnp.maximum(last, 0), some


def shards(
    amp_tiles, amp_row, amp_col, amp_dest, amp_count,
    ladder_ints, ladder_present, cycle_ints, cycle_present,
):
    me = lax.axis_index("pair")
    y, z = me // NZ, me % NZ
    slots = jnp.arange(SLOTS)
    active = slots[None, :] < amp_count[:, None]
    owner = amp_dest // 2

    in_row = lax.dynamic_slice_in_dim(jnp.where(active, owner, -1), y * NZ, NZ, 0)
    goal = jnp.arange(NY) * NZ + z
    hit = (in_row[None] == goal[:, None, None]).astype(jnp.int32)
    rank = jnp.cumsum(hit, axis=2)
    first = [jnp.sum(jnp.where((hit > 0) & (rank == k + 1), slots, 0), axis=2) for k in range(2)]
    sel = jnp.stack(first, axis=2) + (jnp.arange(NZ) * SLOTS)[None, :, None]

    mine = (active & (owner == me)).astype(jnp.int32)
    rank_in = jnp.cumsum(mine, axis=1)
    place = amp_col * 2 + amp_dest % 2
    key = [
        jnp.sum(jnp.where((mine > 0) & (rank_in == k + 1), place - 48, 0), axis=1) + 48 for k in range(2)]
    order, cont, last, some = chain(jnp.stack(key, axis=1).reshape(-1), 48)

    def row(table):
        return lax.dynamic_index_in_dim(table, me, 0, keepdims=False)

    a_key = jnp.where(row(active), row(amp_row) * NCT + row(amp_col), 48)
    a_order, a_cont, a_last, a_some = chain(a_key, 48)

    smem = pl.BlockSpec(memory_space=pltpu.SMEM)
    vmem = pl.BlockSpec(memory_space=pltpu.VMEM)
    dma = pltpu.SemaphoreType.DMA
    out = jax.ShapeDtypeStruct((2 * TILE, COLS), BF16)
    return pl.pallas_call(
        kernel,
        out_shape=(out, out),
        in_specs=[smem] * 11 + [vmem, vmem, pl.BlockSpec(memory_space=pl.ANY)],
        out_specs=(vmem, vmem),
        scratch_shapes=[
            pltpu.VMEM((2, NCT * TILE, COLS), BF16),
            pltpu.VMEM((NZ * SLOTS, PART, TILE), BF16),
            pltpu.VMEM((96, PART, TILE), BF16),
            pltpu.VMEM((128, PART, TILE), BF16),
            pltpu.VMEM((128, PART, TILE), F32),
            pltpu.VMEM((NCT, TILE, 2 * TILE), BF16),
            pltpu.VMEM((SLOTS, TILE, TILE), BF16),
            pltpu.VMEM((SLOTS, TILE, TILE), F32),
            pltpu.VMEM((2 * TILE, NCT * TILE), BF16),
            pltpu.VMEM((2 * TILE, COLS), F32),
            dma((2,)),
            dma((2, HALF)), dma((2, HALF)), dma((2, HALF)), dma((2, HALF)),
            dma((2, NZ)), dma((2, NZ)), dma((2, NZ)), dma((2, NZ)),
            dma((3,)), dma((3,)), dma((4,)), dma((4,)), dma((5,)), dma((5,)),
        ],
        compiler_params=pltpu.CompilerParams(
            collective_id=0, has_side_effects=True, vmem_limit_bytes=40 * 2**20),
        cost_estimate=pl.CostEstimate(flops=1_300_000_000, bytes_accessed=3_000_000, transcendentals=0),
    )(
        ladder_present.reshape(-1), cycle_present.reshape(-1), sel.reshape(-1),
        order, cont, last, some, a_order, a_cont, a_last, a_some,
        ladder_ints, cycle_ints, amp_tiles,
    )


def solution(mesh):
    placed = (
        P("pair", None, None), P(), P(), P(), P(),
        P("pair", "ints"), P(None, "ints"), P("pair", "ints"), P(None, "ints"),
    )
    return jax.shard_map(
        shards,
        mesh=mesh,
        in_specs=placed,
        out_specs=(P("pair", "ints"), P("pair", "ints")),
        check_vma=False,
    )
```

```python
import jax
import jax.numpy as jnp
from jax import lax
from jax.experimental import pallas as pl
from jax.experimental.pallas import tpu as pltpu
from jax.sharding import PartitionSpec as P

TILE = 128
NCT = 24
SLOTS = 24
NY = 4
NZ = 16
NX = 4
PART = 16
ROWS = 48
COLS = 384
HALF = NZ // 2
DEPTH = NZ * ROWS
LAG = 2
PACE = (15,)
MESH = pl.DeviceIdType.MESH
F32 = jnp.float32
BF16 = jnp.bfloat16
I32 = jnp.int32


def iota(shape, dim):
    return lax.broadcasted_iota(I32, shape, dim)


def chain(down, across, value):
    i, j = iota((128, 128), 0), iota((128, 128), 1)
    tie = down == across
    rank = jnp.sum(jnp.where((across < down) | (tie & (j < i)), 1, 0), axis=1, keepdims=True)
    joined = jnp.max(jnp.where(tie & (j < i), 1, 0), axis=1, keepdims=True)
    here = rank == j
    order = jnp.sum(jnp.where(here, value, 0), axis=0, keepdims=True)
    cont = jnp.sum(jnp.where(here, joined, 0), axis=0, keepdims=True)
    last = jnp.sum(jnp.where(down <= j, 1, 0), axis=0, keepdims=True) - 1
    some = jnp.max(jnp.where(down == j, 1, 0), axis=0, keepdims=True)
    return order, cont, jnp.maximum(last, 0), some


def kernel(
    dest, col, row, count, lp, cp, wl, wr, tiles,
    out_l, out_c,
    w, t, zsend, zrecv, pre, bt, a_src, a_pre, a, acc_l, acc_c,
    dest_v, col_v, row_v, count_v, w_in, lp_s, cp_s, count_s, sel_v, tab_v, sel_s, tab_s,
    loc, zw_s, zw_r, y1_s, y1_r, y2_s, y2_r, ty_s, ty_r, tz_s, tz_r, xs_s, xs_r, co_s, co_r,
):
    p = lax.axis_index("pair")
    i = lax.axis_index("ints")
    y, z = p // NZ, p % NZ
    x, core = i // 2, i % 2

    def at(yy, zz):
        return (lax.rem(yy + NY, NY) * NZ + lax.rem(zz + NZ, NZ), i)

    def at_x(xx):
        return (p, lax.rem(xx + NX, NX) * 2 + core)

    zn = (at(y, z + 1), at(y, z - 1))
    yn = (at(y + 1, z), at(y - 1, z))
    xn = (at_x(x + 1), at_x(x - 1))
    twin = (p, x * 2 + 1 - core)

    pairs = [
        (tiles.at[:, pl.ds(pl.multiple_of(PART * i, PART), PART), :], t.at[pl.ds(y * SLOTS, SLOTS)]),
        (wl, w_in.at[0]), (wr, w_in.at[1]), (lp, lp_s), (cp, cp_s),
        (dest, dest_v), (count, count_s), (count, count_v), (col, col_v), (row, row_v), (tiles, a_src),
    ]
    local = [pltpu.make_async_copy(src, dst, loc.at[n]) for n, (src, dst) in enumerate(pairs)]
    for c in local:
        c.start()

    barrier = pltpu.get_barrier_semaphore()
    greet = [at(y, z + d) for d in range(1, NZ)] + [at(y + d, z) for d in range(1, NY)] + [*xn, twin]
    for dev in greet:
        pl.semaphore_signal(barrier, inc=1, device_id=dev, device_id_type=MESH)

    for c in local[1:5]:
        c.wait()
    for k, present in enumerate((lp_s, cp_s)):
        for g in range(ROWS // PART):
            line = (3 * p + g) // 8
            for n in range(COLS // TILE):
                keep = present[n, line].astype(F32)
                block = w_in[k, g * PART:(g + 1) * PART, n * TILE:(n + 1) * TILE].astype(F32)
                w[k, pl.ds(pl.multiple_of(ROWS * p + g * PART, PART), PART), n * TILE:(n + 1) * TILE] = (
                    block * keep).astype(BF16)

    for c in local[5:7]:
        c.wait()
    for ys in range(NY):
        source = ys * NZ + z
        slot = iota((SLOTS, TILE), 0)
        owner = jnp.sum(
            jnp.where(iota((SLOTS, 64), 1) == source, dest_v[...], 0), axis=1, keepdims=True)
        owner = lax.shift_right_logical(owner, 1)
        hit = (owner == y * NZ + iota((SLOTS, TILE), 1)) & (slot < count_s[0, source])
        first = jnp.min(jnp.where(hit, slot, 99), axis=0, keepdims=True)
        second = jnp.max(jnp.where(hit, slot, 0), axis=0, keepdims=True)
        sel_v[2 * ys:2 * ys + 1, :] = jnp.clip(first, 0, SLOTS - 1) + ys * SLOTS
        sel_v[2 * ys + 1:2 * ys + 2, :] = jnp.clip(second, 0, SLOTS - 1) + ys * SLOTS
    sel_copy = pltpu.make_async_copy(sel_v, sel_s, loc.at[11])
    sel_copy.start()
    local[0].wait()
    pl.semaphore_wait(barrier, len(greet))

    sends = []

    def send(src, dst, ss, rs, dev):
        c = pltpu.make_async_remote_copy(
            src_ref=src, dst_ref=dst, send_sem=ss, recv_sem=rs, device_id=dev, device_id_type=MESH)
        c.start()
        sends.append(c)

    def arrived(buf, ss, rs, dev):
        pltpu.make_async_remote_copy(
            src_ref=buf, dst_ref=buf, send_sem=ss, recv_sem=rs, device_id=dev, device_id_type=MESH).wait_recv()

    def w_at(yy, zz, part=None):
        q = lax.rem(yy + NY, NY) * NZ + lax.rem(zz + NZ, NZ)
        rows = pl.ds(pl.multiple_of(q * ROWS, PART), ROWS)
        if part is None:
            return w.at[:, rows, :]
        return w.at[part, rows, :]

    def t_at(yy):
        return t.at[pl.ds(lax.rem(yy + NY, NY) * SLOTS, SLOTS)]

    def group(g):
        if g == 0:
            return [(0, z)]
        if g == HALF:
            return [(NZ - 1, z - HALF)]
        return [(2 * g - 1, z - g), (2 * g, z + g)]

    def y_forward(g):
        for j, zz in group(g):
            for d in range(2):
                send(w_at(y, zz), w_at(y, zz), y1_s.at[d, j], y1_r.at[d, j], yn[d])

    def y_relay(g):
        for j, zz in group(g):
            for d in range(2):
                yy = y - 1 if d == 0 else y + 1
                arrived(w_at(yy, zz), y1_s.at[d, j], y1_r.at[d, j], yn[d])
                send(w_at(yy, zz, d), w_at(yy, zz, d), y2_s.at[d, j], y2_r.at[d, j], yn[d])

    def z_send(s, d):
        zz = z - s if d == 0 else z + s
        part = d if s == HALF - 1 else None
        send(w_at(y, zz, part), w_at(y, zz, part), zw_s.at[d, s], zw_r.at[d, s], zn[d])

    def z_wait(s, d):
        zz = z - s - 1 if d == 0 else z + s + 1
        part = d if s == HALF - 1 else None
        arrived(w_at(y, zz, part), zw_s.at[d, s], zw_r.at[d, s], zn[d])

    for dy in range(1, NY):
        send(t_at(y), t_at(y), ty_s.at[dy - 1], ty_r.at[dy - 1], at(y + dy, z))
    for d in range(2):
        z_send(0, d)
    y_forward(0)

    for dy in range(1, NY):
        arrived(t_at(y - dy), ty_s.at[dy - 1], ty_r.at[dy - 1], at(y + dy, z))
    sel_copy.wait()

    def choose(zz, _):
        for j in range(8):
            zsend[zz * 8 + j] = t[sel_s[j, zz]]
        return 0

    lax.fori_loop(0, NZ, choose, 0)
    for j in range(8):
        zrecv[z * 8 + j] = zsend[z * 8 + j]

    todo = sorted(range(1, NZ), key=lambda d: (-min(d, NZ - d), d))

    def t_sends(num):
        for d in todo[:num]:
            zz = lax.rem(z + d, NZ)
            send(zsend.at[pl.ds(zz * 8, 8)], zrecv.at[pl.ds(z * 8, 8)], tz_s.at[d - 1], tz_r.at[d - 1], at(y, zz))
        del todo[:num]

    def place_a(j, run):
        run = a_src[tab_s[4, j]].astype(F32) + tab_s[5, j].astype(F32) * run
        a_pre[j] = run
        return run

    def tables():
        for c in local[7:10]:
            c.wait()
        slot = iota((SLOTS, 64), 0)
        to = dest_v[...]
        mine = (slot < count_v[...]) & (lax.shift_right_logical(to, 1) == p)
        first = jnp.min(jnp.where(mine, slot, 99), axis=0, keepdims=True)
        second = jnp.max(jnp.where(mine, slot, -1), axis=0, keepdims=True)
        place = col_v[...] * 2 + (to & 1) - 48
        key0 = jnp.sum(jnp.where(mine & (slot == first), place, 0), axis=0, keepdims=True) + 48
        key1 = jnp.sum(
            jnp.where(mine & (slot == second) & (second > first), place, 0), axis=0, keepdims=True) + 48
        across = jnp.broadcast_to(jnp.concatenate([key0, key1], axis=1), (128, 128))
        n = iota((128, 128), 0)
        value = (n & 15) * 8 + (lax.shift_right_logical(n, 4) & 3) * 2 + lax.shift_right_logical(n, 6)
        rows = list(chain(across.T, across, value))
        own = jnp.sum(
            jnp.where(iota((SLOTS, 64), 1) == p, row_v[...] * NCT + col_v[...], 0),
            axis=1, keepdims=True)
        own = jnp.where(iota((SLOTS, 1), 0) < count_s[0, p], own, 48)
        own = jnp.concatenate([own, jnp.full((128 - SLOTS, 1), 99, I32)], axis=0)
        down = jnp.broadcast_to(own, (128, 128))
        rows += chain(down, down.T, n)
        for n, line in enumerate(rows):
            tab_v[n:n + 1, :] = jnp.clip(line, 0, 127 if n < 4 else SLOTS - 1)
        c = pltpu.make_async_copy(tab_v, tab_s, loc.at[12])
        c.start()
        return c

    for s in range(HALF):
        for d in range(2):
            z_wait(s, d)
            if s + 1 < HALF:
                z_send(s + 1, d)
        y_forward(s + 1)
        t_sends(PACE[min(s, len(PACE) - 1)])
        if s == 0:
            tab_copy = tables()
        if s == 1:
            tab_copy.wait()
            local[10].wait()
            lax.fori_loop(0, SLOTS, place_a, jnp.zeros((TILE, TILE), F32))
        if s in (2, 3):
            r = s - 2
            for c in range(NCT):
                q = r * NCT + c
                a[r * TILE:(r + 1) * TILE, c * TILE:(c + 1) * TILE] = (
                    a_pre[tab_s[6, q]] * tab_s[7, q].astype(F32)).astype(BF16)
        if s >= LAG:
            y_relay(s - LAG)

    for d in range(1, NZ):
        zz = lax.rem(z - d + NZ, NZ)
        arrived(zrecv.at[pl.ds(zz * 8, 8)], tz_s.at[d - 1], tz_r.at[d - 1], at(y, z + d))

    def add_up(j, run):
        run = zrecv[tab_s[0, j]].astype(F32) + tab_s[1, j].astype(F32) * run
        pre[j] = run
        return run

    lax.fori_loop(0, 128, add_up, jnp.zeros((PART, TILE), F32), unroll=8)

    def bt_at(ii, lo=0, num=NCT):
        return bt.at[pl.ds(lo, num), pl.ds(pl.multiple_of(ii * PART, PART), PART), :]

    for q in range(2 * NCT):
        c, r = q // 2, q % 2
        bt[c, pl.ds(pl.multiple_of(i * PART, PART), PART), r * TILE:(r + 1) * TILE] = (
            pre[tab_s[2, q]] * tab_s[3, q].astype(F32)).astype(BF16)

    for d in range(2):
        send(bt_at(i), bt_at(i), xs_s.at[d], xs_r.at[d], xn[d])
    send(bt_at(i), bt_at(i), co_s.at[0], co_r.at[0], twin)

    for g in range(HALF - LAG, HALF):
        y_relay(g)

    half = NCT // 2
    for d in range(2):
        ii = xn[1 - d][1]
        arrived(bt_at(ii), xs_s.at[d], xs_r.at[d], xn[d])
        send(bt_at(ii, d * half, half), bt_at(ii, d * half, half), xs_s.at[2 + d], xs_r.at[2 + d], xn[d])
        send(bt_at(ii), bt_at(ii), co_s.at[1 + d], co_r.at[1 + d], twin)
    y_relay(HALF)

    def ladder(yy, fresh=False):
        yy = lax.rem(yy + NY, NY)
        cut = pl.ds(pl.multiple_of(yy * DEPTH, DEPTH), DEPTH)
        add = jnp.dot(a[:, cut], w[0, cut, :], preferred_element_type=F32)
        acc_l[...] = add if fresh else acc_l[...] + add

    def cycle(yy, fresh=False):
        yy = lax.rem(yy + NY, NY)
        cut = pl.ds(pl.multiple_of(yy * DEPTH, DEPTH), DEPTH)
        part = bt[pl.ds(yy * (DEPTH // TILE), DEPTH // TILE)].reshape(DEPTH, 2 * TILE)
        add = lax.dot_general(part, w[1, cut, :], (((0,), (0,)), ((), ())), preferred_element_type=F32)
        acc_c[...] = add if fresh else acc_c[...] + add

    ladder(y, True)
    far = at_x(x + 2)[1]
    for d in range(2):
        arrived(bt_at(far, d * half, half), xs_s.at[2 + d], xs_r.at[2 + d], xn[d])
        send(bt_at(far, d * half, half), bt_at(far, d * half, half), co_s.at[3 + d], co_r.at[3 + d], twin)
    ladder(y + 1)
    ladder(y - 1)

    def other(ii):
        return lax.div(ii, 2) * 2 + 1 - lax.rem(ii, 2)

    arrived(bt_at(other(i)), co_s.at[0], co_r.at[0], twin)
    for d in range(2):
        arrived(bt_at(other(xn[1 - d][1])), co_s.at[1 + d], co_r.at[1 + d], twin)
    for d in range(2):
        arrived(bt_at(other(far), d * half, half), co_s.at[3 + d], co_r.at[3 + d], twin)
    cycle(y, True)
    cycle(y + 1)
    cycle(y - 1)
    for g in range(HALF + 1):
        for j, zz in group(g):
            for d in range(2):
                arrived(w_at(y + 2, zz, d), y2_s.at[d, j], y2_r.at[d, j], yn[d])
    ladder(y + 2)
    out_l[...] = acc_l[...].astype(BF16)
    cycle(y + 2)
    out_c[...] = acc_c[...].astype(BF16)

    for c in sends:
        c.wait_send()


def shards(
    amp_tiles, amp_row, amp_col, amp_dest, amp_count,
    ladder_ints, ladder_present, cycle_ints, cycle_present,
):
    vmem = pl.BlockSpec(memory_space=pltpu.VMEM)
    dma = pltpu.SemaphoreType.DMA
    out = jax.ShapeDtypeStruct((2 * TILE, COLS), BF16)
    return pl.pallas_call(
        kernel,
        out_shape=(out, out),
        in_specs=[pl.BlockSpec(memory_space=pl.ANY)] * 9,
        out_specs=(vmem, vmem),
        scratch_shapes=[
            pltpu.VMEM((2, NCT * TILE, COLS), BF16),
            pltpu.VMEM((NY * SLOTS, PART, TILE), BF16),
            pltpu.VMEM((128, PART, TILE), BF16),
            pltpu.VMEM((128, PART, TILE), BF16),
            pltpu.VMEM((128, PART, TILE), F32),
            pltpu.VMEM((NCT, TILE, 2 * TILE), BF16),
            pltpu.VMEM((SLOTS, TILE, TILE), BF16),
            pltpu.VMEM((SLOTS, TILE, TILE), F32),
            pltpu.VMEM((2 * TILE, NCT * TILE), BF16),
            pltpu.VMEM((2 * TILE, COLS), F32),
            pltpu.VMEM((2 * TILE, COLS), F32),
            pltpu.VMEM((SLOTS, 64), I32), pltpu.VMEM((SLOTS, 64), I32), pltpu.VMEM((SLOTS, 64), I32),
            pltpu.VMEM((1, 64), I32), pltpu.VMEM((2, ROWS, COLS), BF16),
            pltpu.SMEM((3, NCT), I32), pltpu.SMEM((3, NCT), I32), pltpu.SMEM((1, 64), I32),
            pltpu.VMEM((8, TILE), I32), pltpu.VMEM((8, TILE), I32),
            pltpu.SMEM((8, TILE), I32), pltpu.SMEM((8, TILE), I32),
            dma((13,)),
            dma((2, HALF)), dma((2, HALF)),
            dma((2, NZ)), dma((2, NZ)), dma((2, NZ)), dma((2, NZ)),
            dma((NY - 1,)), dma((NY - 1,)), dma((NZ - 1,)), dma((NZ - 1,)),
            dma((4,)), dma((4,)), dma((5,)), dma((5,)),
        ],
        compiler_params=pltpu.CompilerParams(
            collective_id=0, has_side_effects=True, vmem_limit_bytes=56 * 2**20),
        cost_estimate=pl.CostEstimate(flops=1_300_000_000, bytes_accessed=3_000_000, transcendentals=0),
    )(
        amp_dest.T, amp_col.T, amp_row.T, amp_count.reshape(1, -1), ladder_present.T, cycle_present.T,
        ladder_ints, cycle_ints, amp_tiles,
    )


def solution(mesh):
    placed = (
        P("pair", None, None), P(), P(), P(), P(),
        P("pair", "ints"), P(None, "ints"), P("pair", "ints"), P(None, "ints"),
    )
    return jax.shard_map(
        shards,
        mesh=mesh,
        in_specs=placed,
        out_specs=(P("pair", "ints"), P("pair", "ints")),
        check_vma=False,
    )
```

```python
import jax
import jax.numpy as jnp
from jax import lax
from jax.experimental import pallas as pl
from jax.experimental.pallas import tpu as pltpu
from jax.sharding import PartitionSpec as P

TILE = 128
NCT = 24
SLOTS = 24
NY = 4
NZ = 16
NX = 4
PART = 16
ROWS = 48
COLS = 384
DEPTH = NZ * ROWS
LAG = 4
W_REACH = (8, 7)
T_REACH = (7, 8)
CUTS = 2
RIM_OUT = (2, 4, 6, 9, 11, 13)
ROOM = 56
MESH = pl.DeviceIdType.MESH
F32 = jnp.float32
BF16 = jnp.bfloat16
I32 = jnp.int32


def iota(shape, dim):
    return lax.broadcasted_iota(I32, shape, dim)


def chain(down, across, value):
    i, j = iota((128, 128), 0), iota((128, 128), 1)
    tie = down == across
    rank = jnp.sum(jnp.where((across < down) | (tie & (j < i)), 1, 0), axis=1, keepdims=True)
    joined = jnp.max(jnp.where(tie & (j < i), 1, 0), axis=1, keepdims=True)
    here = rank == j
    order = jnp.sum(jnp.where(here, value, 0), axis=0, keepdims=True)
    cont = jnp.sum(jnp.where(here, joined, 0), axis=0, keepdims=True)
    last = jnp.sum(jnp.where(down <= j, 1, 0), axis=0, keepdims=True) - 1
    some = jnp.max(jnp.where(down == j, 1, 0), axis=0, keepdims=True)
    return order, cont, jnp.maximum(last, 0), some


def kernel(
    dest, col, row, count, lp, cp, wl, wr, tiles,
    out_l, out_c,
    w, ysend, yrecv, pre, bt, a_src, a_pre, a, acc_l, acc_c, acc_p, from_mate, ams, ams_pre, am,
    dest_v, col_v, row_v, count_v, w_in, lp_s, cp_s, count_s, sel_v, tab_v, sel_s, tab_s,
    loc, zw_s, zw_r, y1_s, y1_r, y2_s, y2_r, ty_s, ty_r, tz_s, tz_r, xs_s, xs_r, co_s, co_r,
    ax_s, ax_r, ac_s, ac_r, ay_s, ay_r, pc_s, pc_r, *t,
):
    p = lax.axis_index("pair")
    i = lax.axis_index("ints")
    y, z = p // NZ, p % NZ
    x, core = i // 2, i % 2

    def at(yy, zz):
        return (lax.rem(yy + NY, NY) * NZ + lax.rem(zz + NZ, NZ), i)

    def at_x(xx):
        return (p, lax.rem(xx + NX, NX) * 2 + core)

    zn = (at(y, z + 1), at(y, z - 1))
    odd = lax.rem(y, 2)
    ym, yr, yf = y + 1 - 2 * odd, lax.rem(y + 3 + 2 * odd, NY), lax.rem(y + 2, NY)
    yn = (at(ym, z), at(yr, z))
    xn = (at_x(x + 1), at_x(x - 1))
    twin = (p, x * 2 + 1 - core)

    pairs = [
        (tiles.at[:, pl.ds(pl.multiple_of(PART * i, PART), PART), :], t[0]),
        (wl, w_in.at[0]), (wr, w_in.at[1]), (lp, lp_s), (cp, cp_s),
        (dest, dest_v), (count, count_s), (count, count_v), (col, col_v), (row, row_v), (tiles, a_src),
    ]
    local = [pltpu.make_async_copy(src, dst, loc.at[n]) for n, (src, dst) in enumerate(pairs)]
    for c in local:
        c.start()

    barrier = pltpu.get_barrier_semaphore()
    greet = [*zn, *xn, twin] + [at(y + d, z) for d in range(1, NY)]
    for dev in greet:
        pl.semaphore_signal(barrier, inc=1, device_id=dev, device_id_type=MESH)

    sends = []

    def send(src, dst, ss, rs, dev):
        c = pltpu.make_async_remote_copy(
            src_ref=src, dst_ref=dst, send_sem=ss, recv_sem=rs, device_id=dev, device_id_type=MESH)
        c.start()
        sends.append(c)

    def arrived(buf, ss, rs, dev):
        pltpu.make_async_remote_copy(
            src_ref=buf, dst_ref=buf, send_sem=ss, recv_sem=rs, device_id=dev, device_id_type=MESH).wait_recv()

    def w_at(yy, zz, part=None):
        q = lax.rem(yy + NY, NY) * NZ + lax.rem(zz + NZ, NZ)
        rows = pl.ds(pl.multiple_of(q * ROWS, PART), ROWS)
        if part is None:
            return w.at[:, rows, :]
        return w.at[part, rows, :]

    def t_send(s, d, h):
        if s < T_REACH[d]:
            cut = pl.ds(h * (SLOTS // CUTS), SLOTS // CUTS)
            here, there = ((NZ - s) % NZ, NZ - s - 1) if d == 0 else (s, s + 1)
            src = t[here].at[cut]
            if s == 0:
                src = tiles.at[cut, pl.ds(pl.multiple_of(PART * i, PART), PART), :]
            send(src, t[there].at[cut], tz_s.at[d, s * CUTS + h], tz_r.at[d, s * CUTS + h], zn[d])

    def t_wait(s, d, h):
        if s < T_REACH[d]:
            cut = pl.ds(h * (SLOTS // CUTS), SLOTS // CUTS)
            arrived(t[NZ - s - 1 if d == 0 else s + 1].at[cut], tz_s.at[d, s * CUTS + h], tz_r.at[d, s * CUTS + h], zn[d])

    pl.semaphore_wait(barrier, len(greet))
    for h in range(CUTS):
        for d in range(2):
            t_send(0, d, h)

    for c in local[1:5]:
        c.wait()
    for k, present in enumerate((lp_s, cp_s)):
        for g in range(ROWS // PART):
            line = (3 * p + g) // 8
            for n in range(COLS // TILE):
                keep = present[n, line].astype(F32)
                block = w_in[k, g * PART:(g + 1) * PART, n * TILE:(n + 1) * TILE].astype(F32)
                w[k, pl.ds(pl.multiple_of(ROWS * p + g * PART, PART), PART), n * TILE:(n + 1) * TILE] = (
                    block * keep).astype(BF16)

    reach = W_REACH
    steps = NZ // 2

    def group(g):
        if g == 0:
            return [(0, z)]
        near = [(NZ - g, z - g)] if g <= reach[0] else []
        return near + ([(g, z + g)] if g <= reach[1] else [])

    def y_forward(g):
        for j, zz in group(g):
            send(w_at(y, zz), w_at(y, zz), y1_s.at[1, j], y1_r.at[1, j], yn[1])
            send(w_at(y, zz, 1), w_at(y, zz, 1), y1_s.at[0, j], y1_r.at[0, j], yn[0])

    def y_relay(g):
        for j, zz in group(g):
            arrived(w_at(yr, zz), y1_s.at[1, j], y1_r.at[1, j], yn[1])
            arrived(w_at(ym, zz, 1), y1_s.at[0, j], y1_r.at[0, j], yn[0])
            e = int(j in RIM_OUT)
            part = w_at(ym if e else yr, zz, 1)
            send(part, part, y2_s.at[j], y2_r.at[j], yn[e])

    def z_send(s, d, k):
        zz = z - s if d == 0 else z + s
        if s < reach[d]:
            send(w_at(y, zz, k), w_at(y, zz, k), zw_s.at[d, 2 * s + k], zw_r.at[d, 2 * s + k], zn[d])

    def z_wait(s, d, k):
        zz = z - s - 1 if d == 0 else z + s + 1
        if s < reach[d]:
            arrived(w_at(y, zz, k), zw_s.at[d, 2 * s + k], zw_r.at[d, 2 * s + k], zn[d])

    for k in range(2):
        for d in range(2):
            z_send(0, d, k)
    y_forward(0)

    for c in local[5:8:2]:
        c.wait()
    slot = iota((SLOTS, 64), 0)
    used = slot < count_v[...]
    owner = lax.shift_right_logical(dest_v[...], 1)
    for yy in range(NY):
        hit = used & (owner == yy * NZ + z)
        first = jnp.min(jnp.where(hit, slot, SLOTS - 1), axis=0, keepdims=True)
        second = jnp.max(jnp.where(hit, slot, 0), axis=0, keepdims=True)
        sel_v[2 * yy:2 * yy + 1, :] = jnp.clip(first, 0, SLOTS - 1)
        sel_v[2 * yy + 1:2 * yy + 2, :] = jnp.clip(second, 0, SLOTS - 1)
    sel_copy = pltpu.make_async_copy(sel_v, sel_s, loc.at[11])
    sel_copy.start()
    local[0].wait()
    sel_copy.wait()

    def span(g):
        return (0, 1) if g == 0 else (NZ - 1, 1) if g == NZ // 2 else (2 * g - 1, 2)

    def y_piece(buf, dy, g):
        lo, num = span(g)
        return buf.at[pl.ds((dy * NZ + lo) * 2, num * 2)]

    def choose(g):
        far = [g] if g in (0, NZ // 2) else [NZ - g, g]
        for n, zz in enumerate([z + o for o in far]):
            zz = lax.rem(zz + NZ, NZ)
            for dy in (1, 2, 3, 0):
                yy = lax.rem(y + dy, NY)
                for j in range(2):
                    buf, row = (ysend, dy - 1) if dy else (yrecv, 0)
                    buf[(row * NZ + span(g)[0] + n) * 2 + j] = t[far[n]][sel_s[2 * yy + j, y * NZ + zz]]
        for dy in (1, 3, 2):
            send(y_piece(ysend, dy - 1, g), y_piece(yrecv, dy, g),
                 ty_s.at[dy - 1, g], ty_r.at[dy - 1, g], at(y + dy, z))

    choose(0)

    def place_a(j, run):
        run = a_src[tab_s[4, j]].astype(F32) + tab_s[5, j].astype(F32) * run
        a_pre[j] = run
        return run

    def place_slices(j, run):
        run = t[0][tab_s[4, j]].astype(F32) + tab_s[5, j].astype(F32) * run
        ams_pre[j] = run
        return run

    def a_place(buf, r, c, first, second):
        q = r * NCT + (first * 6 + c if c < 6 else second * 6 + c - 6)
        return (buf[tab_s[6, q]] * tab_s[7, q].astype(F32)).astype(BF16)

    def part_rows(ii):
        return pl.ds(pl.multiple_of(ii * PART, PART), PART)

    def other(ii):
        return lax.div(ii, 2) * 2 + 1 - lax.rem(ii, 2)

    def spread(piece, xs, xr, cs, cr):
        def start():
            for n in range(2):
                for d in range(2):
                    send(piece(i, (d + n) % 2), piece(i, (d + n) % 2), xs.at[d, n], xr.at[d, n], xn[d])
            for h in range(2):
                send(piece(i, h), piece(i, h), cs.at[h], cr.at[h], twin)

        def near():
            for n in range(2):
                for d in range(2):
                    part = piece(xn[1 - d][1], (d + n) % 2)
                    arrived(part, xs.at[d, n], xr.at[d, n], xn[d])
                    if n == 0:
                        send(part, part, xs.at[d, 2], xr.at[d, 2], xn[d])
                    send(part, part, cs.at[2 + 2 * n + d], cr.at[2 + 2 * n + d], twin)

        def last():
            for d in range(2):
                part = piece(at_x(x + 2)[1], d)
                arrived(part, xs.at[d, 2], xr.at[d, 2], xn[d])
                send(part, part, cs.at[6 + d], cr.at[6 + d], twin)

        def finish():
            for h in range(2):
                arrived(piece(other(i), h), cs.at[h], cr.at[h], twin)
            for n in range(2):
                for d in range(2):
                    part = piece(other(xn[1 - d][1]), (d + n) % 2)
                    arrived(part, cs.at[2 + 2 * n + d], cr.at[2 + 2 * n + d], twin)
            for d in range(2):
                arrived(piece(other(at_x(x + 2)[1]), d), cs.at[6 + d], cr.at[6 + d], twin)

        return start, near, last, finish

    am_spread = spread(lambda ii, h: am.at[h, part_rows(ii), :], ax_s, ax_r, ac_s, ac_r)
    half = NCT // 2
    bt_spread = spread(lambda ii, h: bt.at[pl.ds(h * half, half), part_rows(ii), :], xs_s, xs_r, co_s, co_r)

    def tables():
        for c in (local[6], *local[8:10]):
            c.wait()
        to = dest_v[...]
        mine = used & (owner == p)
        first = jnp.min(jnp.where(mine, slot, 99), axis=0, keepdims=True)
        second = jnp.max(jnp.where(mine, slot, -1), axis=0, keepdims=True)
        place = col_v[...] * 2 + (to & 1) - 48
        key0 = jnp.sum(jnp.where(mine & (slot == first), place, 0), axis=0, keepdims=True) + 48
        key1 = jnp.sum(
            jnp.where(mine & (slot == second) & (second > first), place, 0), axis=0, keepdims=True) + 48
        across = jnp.broadcast_to(jnp.concatenate([key0, key1], axis=1), (128, 128))
        n = iota((128, 128), 0)
        dy = (y + NY - lax.shift_right_logical(n, 4)) & 3
        off = (n + NZ - z) & 15
        turn = jnp.where(off < 8, 2 * off, jnp.where(off == 8, NZ - 1, 31 - 2 * off))
        value = dy * 32 + turn * 2 + lax.shift_right_logical(n, 6)
        rows = list(chain(across.T, across, value))
        own = jnp.sum(
            jnp.where(iota((SLOTS, 64), 1) == p, row_v[...] * NCT + col_v[...], 0),
            axis=1, keepdims=True)
        own = jnp.where(iota((SLOTS, 1), 0) < count_s[0, p], own, 48)
        own = jnp.concatenate([own, jnp.full((128 - SLOTS, 1), 99, I32)], axis=0)
        down = jnp.broadcast_to(own, (128, 128))
        rows += chain(down, down.T, n)
        for n, line in enumerate(rows):
            tab_v[n:n + 1, :] = jnp.clip(line, 0, 127 if n < 4 else SLOTS - 1)
        c = pltpu.make_async_copy(tab_v, tab_s, loc.at[12])
        c.start()
        return c

    for s in range(steps):
        for k in range(2):
            for d in range(2):
                t_wait(s, d, k)
                t_send(s + 1, d, k)
            for d in range(2):
                z_wait(s, d, k)
                z_send(s + 1, d, k)
        choose(s + 1)
        y_forward(s + 1)
        if s == 0:
            tab_copy = tables()
        if s == 1:
            tab_copy.wait()
            lax.fori_loop(0, SLOTS, place_slices, jnp.zeros((PART, TILE), F32))
            for r in range(2):
                for c in range(12):
                    ams[r, :, c * TILE:(c + 1) * TILE] = a_place(ams_pre, r, c, ym, yf)
            send(ams, am.at[:, part_rows(i), :], ay_s.at[0], ay_r.at[0], yn[0])
        if s == 2:
            local[10].wait()
            lax.fori_loop(0, SLOTS, place_a, jnp.zeros((TILE, TILE), F32))
        if s == 3:
            arrived(am.at[:, part_rows(i), :], ay_s.at[0], ay_r.at[0], yn[0])
            am_spread[0]()
            for r in range(2):
                for c in range(12):
                    a[r * TILE:(r + 1) * TILE, c * TILE:(c + 1) * TILE] = a_place(a_pre, r, c, y, yr)
        if s == 5:
            am_spread[1]()
        if s == 7:
            am_spread[2]()
        if s >= LAG:
            y_relay(s - LAG)

    for g in range(steps + 1):
        for dy in (1, 3, 2):
            arrived(y_piece(yrecv, dy, g), ty_s.at[dy - 1, g], ty_r.at[dy - 1, g], at(y + dy, z))

    def add_up(j, run):
        run = yrecv[tab_s[0, j]].astype(F32) + tab_s[1, j].astype(F32) * run
        pre[j] = run
        return run

    lax.fori_loop(0, 128, add_up, jnp.zeros((PART, TILE), F32), unroll=8)

    for q in range(2 * NCT):
        c, r = q // 2, q % 2
        bt[c, part_rows(i), r * TILE:(r + 1) * TILE] = (pre[tab_s[2, q]] * tab_s[3, q].astype(F32)).astype(BF16)

    bt_spread[0]()
    for g in range(steps - LAG, steps + 1):
        y_relay(g)

    am_spread[3]()

    def wl_rows(yy):
        return w[0, pl.ds(pl.multiple_of(yy * DEPTH, DEPTH), DEPTH), :]

    def half_ladder(buf, acc):
        for n, yy in enumerate((y, yr)):
            left = buf[..., n * DEPTH:(n + 1) * DEPTH].reshape(2 * TILE, DEPTH)
            add = jnp.dot(left, wl_rows(yy), preferred_element_type=F32)
            acc[...] = acc[...] + add if n else add

    half_ladder(am, acc_p)
    send(acc_p, from_mate, pc_s.at[0], pc_r.at[0], yn[0])
    bt_spread[1]()
    half_ladder(a, acc_l)
    bt_spread[2]()

    def cycle(yy, fresh=False):
        cut = pl.ds(pl.multiple_of(yy * DEPTH, DEPTH), DEPTH)
        part = bt[pl.ds(yy * (DEPTH // TILE), DEPTH // TILE)].reshape(DEPTH, 2 * TILE)
        add = lax.dot_general(part, w[1, cut, :], (((0,), (0,)), ((), ())), preferred_element_type=F32)
        acc_c[...] = add if fresh else acc_c[...] + add

    bt_spread[3]()
    cycle(y, True)
    cycle(ym)
    cycle(yr)
    for g in range(steps + 1):
        for j, zz in group(g):
            arrived(w_at(yf, zz, 1), y2_s.at[j], y2_r.at[j], yn[int(j in RIM_OUT)])
    cycle(yf)
    out_c[...] = acc_c[...].astype(BF16)
    arrived(from_mate, pc_s.at[0], pc_r.at[0], yn[0])
    out_l[...] = (acc_l[...] + from_mate[...]).astype(BF16)

    for c in sends:
        c.wait_send()


def shards(
    amp_tiles, amp_row, amp_col, amp_dest, amp_count,
    ladder_ints, ladder_present, cycle_ints, cycle_present,
):
    vmem, anywhere = pl.BlockSpec(memory_space=pltpu.VMEM), pl.BlockSpec(memory_space=pl.ANY)
    dma = pltpu.SemaphoreType.DMA
    out = jax.ShapeDtypeStruct((2 * TILE, COLS), BF16)
    return pl.pallas_call(
        kernel,
        out_shape=(out, out),
        in_specs=[anywhere] * 9,
        out_specs=(vmem, vmem),
        scratch_shapes=[
            pltpu.VMEM((2, NCT * TILE, COLS), BF16),
            pltpu.VMEM((96, PART, TILE), BF16),
            pltpu.VMEM((128, PART, TILE), BF16),
            pltpu.VMEM((128, PART, TILE), F32),
            pltpu.VMEM((NCT, TILE, 2 * TILE), BF16),
            pltpu.VMEM((SLOTS, TILE, TILE), BF16),
            pltpu.VMEM((SLOTS, TILE, TILE), F32),
            pltpu.VMEM((2 * TILE, 2 * DEPTH), BF16),
            *[pltpu.VMEM((2 * TILE, COLS), F32)] * 4,
            pltpu.VMEM((2, PART, 2 * DEPTH), BF16),
            pltpu.VMEM((SLOTS, PART, TILE), F32),
            pltpu.VMEM((2, TILE, 2 * DEPTH), BF16),
            pltpu.VMEM((SLOTS, 64), I32), pltpu.VMEM((SLOTS, 64), I32), pltpu.VMEM((SLOTS, 64), I32),
            pltpu.VMEM((1, 64), I32), pltpu.VMEM((2, ROWS, COLS), BF16),
            pltpu.SMEM((3, NCT), I32), pltpu.SMEM((3, NCT), I32), pltpu.SMEM((1, 64), I32),
            pltpu.VMEM((8, 64), I32), pltpu.VMEM((8, TILE), I32),
            pltpu.SMEM((8, 64), I32), pltpu.SMEM((8, TILE), I32),
            dma((13,)),
            dma((2, 2 * NZ)), dma((2, 2 * NZ)),
            dma((2, NZ)), dma((2, NZ)), dma((NZ,)), dma((NZ,)),
            dma((NY - 1, 9)), dma((NY - 1, 9)), dma((2, 8 * CUTS)), dma((2, 8 * CUTS)),
            dma((2, 3)), dma((2, 3)), dma((8,)), dma((8,)), dma((2, 3)), dma((2, 3)), dma((8,)), dma((8,)),
            dma((1,)), dma((1,)), dma((1,)), dma((1,)),
            *[pltpu.VMEM((SLOTS, PART, TILE), BF16)] * NZ,
        ],
        compiler_params=pltpu.CompilerParams(
            collective_id=0, has_side_effects=True, vmem_limit_bytes=ROOM * 2**20),
        cost_estimate=pl.CostEstimate(flops=1_300_000_000, bytes_accessed=3_000_000, transcendentals=0),
    )(
        amp_dest.T, amp_col.T, amp_row.T, amp_count.reshape(1, -1), ladder_present.T, cycle_present.T,
        ladder_ints, cycle_ints, amp_tiles,
    )


def solution(mesh):
    placed = (
        P("pair", None, None), P(), P(), P(), P(),
        P("pair", "ints"), P(None, "ints"), P("pair", "ints"), P(None, "ints"),
    )
    return jax.shard_map(
        shards,
        mesh=mesh,
        in_specs=placed,
        out_specs=(P("pair", "ints"), P("pair", "ints")),
        check_vma=False,
    )
```

```python
import jax
import jax.numpy as jnp
from jax import lax
from jax.experimental import pallas as pl
from jax.experimental.pallas import tpu as pltpu
from jax.sharding import PartitionSpec as P

TILE = 128
NCT = 24
SLOTS = 24
NY = 4
NZ = 16
NX = 4
PART = 16
ROWS = 48
COLS = 384
DEPTH = NZ * ROWS
LAG = 4
W_REACH = (8, 7)
T_REACH = (7, 8)
LAST = (NZ - T_REACH[0], T_REACH[1])
CUTS = 2
BEHIND = 0
RIM_OUT = (3, 5, 6, 7, 8, 9, 11, 13)
ROOM = 56
MESH = pl.DeviceIdType.MESH
F32 = jnp.float32
BF16 = jnp.bfloat16
I32 = jnp.int32


def iota(shape, dim):
    return lax.broadcasted_iota(I32, shape, dim)


def chain(down, across, value):
    i, j = iota((128, 128), 0), iota((128, 128), 1)
    tie = down == across
    rank = jnp.sum(jnp.where((across < down) | (tie & (j < i)), 1, 0), axis=1, keepdims=True)
    joined = jnp.max(jnp.where(tie & (j < i), 1, 0), axis=1, keepdims=True)
    here = rank == j
    order = jnp.sum(jnp.where(here, value, 0), axis=0, keepdims=True)
    cont = jnp.sum(jnp.where(here, joined, 0), axis=0, keepdims=True)
    last = jnp.sum(jnp.where(down <= j, 1, 0), axis=0, keepdims=True) - 1
    some = jnp.max(jnp.where(down == j, 1, 0), axis=0, keepdims=True)
    return order, cont, jnp.maximum(last, 0), some


def kernel(
    dest, col, row, count, lp, cp, wl, wr, tiles,
    out_l, out_c,
    w, ysend, yrecv, pre, bt, a_src, a_pre, a, acc_l, acc_c, acc_p, from_mate, ams, ams_pre, am,
    dest_v, col_v, row_v, count_v, w_in, lp_s, cp_s, count_s, sel_v, tab_v, sel_s, tab_s, next_v, next_s,
    loc, zw_s, zw_r, y1_s, y1_r, y2_s, y2_r, ty_s, ty_r, tz_s, tz_r, xs_s, xs_r, co_s, co_r,
    ax_s, ax_r, ac_s, ac_r, ay_s, ay_r, pc_s, pc_r, *t,
):
    p = lax.axis_index("pair")
    i = lax.axis_index("ints")
    y, z = p // NZ, p % NZ
    x, core = i // 2, i % 2

    def at(yy, zz):
        return (lax.rem(yy + NY, NY) * NZ + lax.rem(zz + NZ, NZ), i)

    def at_x(xx):
        return (p, lax.rem(xx + NX, NX) * 2 + core)

    zn = (at(y, z + 1), at(y, z - 1))
    odd = lax.rem(y, 2)
    ym, yr, yf = y + 1 - 2 * odd, lax.rem(y + 3 + 2 * odd, NY), lax.rem(y + 2, NY)
    yn = (at(ym, z), at(yr, z))
    xn = (at_x(x + 1), at_x(x - 1))
    twin = (p, x * 2 + 1 - core)

    pairs = [
        (tiles.at[:, pl.ds(pl.multiple_of(PART * i, PART), PART), :], t[0]),
        (wl, w_in.at[0]), (wr, w_in.at[1]), (lp, lp_s), (cp, cp_s),
        (dest, dest_v), (count, count_s), (count, count_v), (col, col_v), (row, row_v), (tiles, a_src),
    ]
    local = [pltpu.make_async_copy(src, dst, loc.at[n]) for n, (src, dst) in enumerate(pairs)]
    for c in local:
        c.start()

    barrier = pltpu.get_barrier_semaphore()
    greet = [*zn, *xn, twin] + [at(y + d, z) for d in range(1, NY)]
    for dev in greet:
        pl.semaphore_signal(barrier, inc=1, device_id=dev, device_id_type=MESH)

    sends = []

    def send(src, dst, ss, rs, dev):
        c = pltpu.make_async_remote_copy(
            src_ref=src, dst_ref=dst, send_sem=ss, recv_sem=rs, device_id=dev, device_id_type=MESH)
        c.start()
        sends.append(c)

    def arrived(buf, ss, rs, dev):
        pltpu.make_async_remote_copy(
            src_ref=buf, dst_ref=buf, send_sem=ss, recv_sem=rs, device_id=dev, device_id_type=MESH).wait_recv()

    def w_at(yy, zz, part=None):
        q = lax.rem(yy + NY, NY) * NZ + lax.rem(zz + NZ, NZ)
        rows = pl.ds(pl.multiple_of(q * ROWS, PART), ROWS)
        if part is None:
            return w.at[:, rows, :]
        return w.at[part, rows, :]

    def t_send(s, d, h):
        cut = pl.ds(h * (SLOTS // CUTS), SLOTS // CUTS)
        here, there = ((NZ - s) % NZ, NZ - s - 1) if d == 0 else (s, s + 1)
        if s == T_REACH[d] - 1 and h == CUTS - 1:
            zz = lax.rem(z + here, NZ)
            for q in range(8):
                t[18 + d][q] = t[here][next_s[8 * d + q, y * NZ + zz]]
            send(t[18 + d], t[16 + d], tz_s.at[d, s * CUTS], tz_r.at[d, s * CUTS], zn[d])
        elif s < T_REACH[d] - 1:
            src = t[here].at[cut]
            if s == 0:
                src = tiles.at[cut, pl.ds(pl.multiple_of(PART * i, PART), PART), :]
            send(src, t[there].at[cut], tz_s.at[d, s * CUTS + h], tz_r.at[d, s * CUTS + h], zn[d])

    def t_wait(s, d, h):
        if s == T_REACH[d] - 1 and h == CUTS - 1:
            arrived(t[16 + d], tz_s.at[d, s * CUTS], tz_r.at[d, s * CUTS], zn[d])
        elif s < T_REACH[d] - 1:
            cut = pl.ds(h * (SLOTS // CUTS), SLOTS // CUTS)
            arrived(t[NZ - s - 1 if d == 0 else s + 1].at[cut], tz_s.at[d, s * CUTS + h], tz_r.at[d, s * CUTS + h], zn[d])

    pl.semaphore_wait(barrier, len(greet))
    for h in range(CUTS):
        for d in range(2):
            t_send(0, d, h)

    for c in local[1:5]:
        c.wait()
    for k, present in enumerate((lp_s, cp_s)):
        for g in range(ROWS // PART):
            line = (3 * p + g) // 8
            for n in range(COLS // TILE):
                keep = present[n, line].astype(F32)
                block = w_in[k, g * PART:(g + 1) * PART, n * TILE:(n + 1) * TILE].astype(F32)
                w[k, pl.ds(pl.multiple_of(ROWS * p + g * PART, PART), PART), n * TILE:(n + 1) * TILE] = (
                    block * keep).astype(BF16)

    reach = W_REACH
    steps = NZ // 2

    def group(g):
        if g == 0:
            return [(0, z)]
        near = [(NZ - g, z - g)] if g <= reach[0] else []
        return near + ([(g, z + g)] if g <= reach[1] else [])

    def y_forward(g):
        for j, zz in group(g):
            send(w_at(y, zz, 1), w_at(y, zz, 1), y1_s.at[1, j], y1_r.at[1, j], yn[1])
            send(w_at(y, zz, 1), w_at(y, zz, 1), y1_s.at[0, j], y1_r.at[0, j], yn[0])
            send(w_at(y, zz, 0), w_at(y, zz, 0), y1_s.at[2, j], y1_r.at[2, j], yn[1])

    def y_relay(g):
        for j, zz in group(g):
            arrived(w_at(yr, zz, 1), y1_s.at[1, j], y1_r.at[1, j], yn[1])
            arrived(w_at(ym, zz, 1), y1_s.at[0, j], y1_r.at[0, j], yn[0])
            e = int(j in RIM_OUT)
            part = w_at(ym if e else yr, zz, 1)
            send(part, part, y2_s.at[j], y2_r.at[j], yn[e])

    def z_send(s, d, k):
        zz = z - s if d == 0 else z + s
        if s < reach[d]:
            send(w_at(y, zz, k), w_at(y, zz, k), zw_s.at[d, 2 * s + k], zw_r.at[d, 2 * s + k], zn[d])

    def z_wait(s, d, k):
        zz = z - s - 1 if d == 0 else z + s + 1
        if s < reach[d]:
            arrived(w_at(y, zz, k), zw_s.at[d, 2 * s + k], zw_r.at[d, 2 * s + k], zn[d])

    for k in range(2):
        for d in range(2):
            z_send(0, d, k)
    y_forward(0)

    for c in local[5:8:2]:
        c.wait()
    slot = iota((SLOTS, 64), 0)
    used = slot < count_v[...]
    owner = lax.shift_right_logical(dest_v[...], 1)

    def pick(table, lo, zz):
        for yy in range(NY):
            hit = used & (owner == yy * NZ + zz)
            first = jnp.min(jnp.where(hit, slot, SLOTS - 1), axis=0, keepdims=True)
            second = jnp.max(jnp.where(hit, slot, 0), axis=0, keepdims=True)
            table[lo + 2 * yy:lo + 2 * yy + 1, :] = jnp.clip(first, 0, SLOTS - 1)
            table[lo + 2 * yy + 1:lo + 2 * yy + 2, :] = jnp.clip(second, 0, SLOTS - 1)

    pick(sel_v, 0, z)
    sel_copy = pltpu.make_async_copy(sel_v, sel_s, loc.at[11])
    sel_copy.start()
    local[0].wait()
    sel_copy.wait()

    def span(g):
        return (0, 1) if g == 0 else (NZ - 1, 1) if g == NZ // 2 else (2 * g - 1, 2)

    def y_piece(buf, dy, g):
        lo, num = span(g)
        return buf.at[pl.ds((dy * NZ + lo) * 2, num * 2)]

    def choose(g):
        far = [g] if g in (0, NZ // 2) else [NZ - g, g]
        for n, zz in enumerate([z + o for o in far]):
            zz = lax.rem(zz + NZ, NZ)
            for dy in (1, 2, 3, 0):
                yy = lax.rem(y + dy, NY)
                for j in range(2):
                    buf, row = (ysend, dy - 1) if dy else (yrecv, 0)
                    if far[n] in LAST:
                        tile = t[16 + LAST.index(far[n])][2 * yy + j]
                    else:
                        tile = t[far[n]][sel_s[2 * yy + j, y * NZ + zz]]
                    buf[(row * NZ + span(g)[0] + n) * 2 + j] = tile
        for dy in (1, 3, 2):
            send(y_piece(ysend, dy - 1, g), y_piece(yrecv, dy, g),
                 ty_s.at[dy - 1, g], ty_r.at[dy - 1, g], at(y + dy, z))

    choose(0)

    def place_a(j, run):
        run = a_src[tab_s[4, j]].astype(F32) + tab_s[5, j].astype(F32) * run
        a_pre[j] = run
        return run

    def place_slices(j, run):
        run = t[0][tab_s[4, j]].astype(F32) + tab_s[5, j].astype(F32) * run
        ams_pre[j] = run
        return run

    def a_place(buf, r, c, first, second):
        q = r * NCT + (first * 6 + c if c < 6 else second * 6 + c - 6)
        return (buf[tab_s[6, q]] * tab_s[7, q].astype(F32)).astype(BF16)

    def part_rows(ii):
        return pl.ds(pl.multiple_of(ii * PART, PART), PART)

    def other(ii):
        return lax.div(ii, 2) * 2 + 1 - lax.rem(ii, 2)

    def spread(piece, xs, xr, cs, cr):
        def start():
            for n in range(2):
                for d in range(2):
                    send(piece(i, (d + n) % 2), piece(i, (d + n) % 2), xs.at[d, n], xr.at[d, n], xn[d])
            for h in range(2):
                send(piece(i, h), piece(i, h), cs.at[h], cr.at[h], twin)

        def near():
            for n in range(2):
                for d in range(2):
                    part = piece(xn[1 - d][1], (d + n) % 2)
                    arrived(part, xs.at[d, n], xr.at[d, n], xn[d])
                    if n == 0:
                        send(part, part, xs.at[d, 2], xr.at[d, 2], xn[d])
                    send(part, part, cs.at[2 + 2 * n + d], cr.at[2 + 2 * n + d], twin)

        def last():
            for d in range(2):
                part = piece(at_x(x + 2)[1], d)
                arrived(part, xs.at[d, 2], xr.at[d, 2], xn[d])
                send(part, part, cs.at[6 + d], cr.at[6 + d], twin)

        def own_in():
            for h in range(2):
                arrived(piece(other(i), h), cs.at[h], cr.at[h], twin)

        def near_in():
            for n in range(2):
                for d in range(2):
                    part = piece(other(xn[1 - d][1]), (d + n) % 2)
                    arrived(part, cs.at[2 + 2 * n + d], cr.at[2 + 2 * n + d], twin)

        def last_in():
            for d in range(2):
                arrived(piece(other(at_x(x + 2)[1]), d), cs.at[6 + d], cr.at[6 + d], twin)

        return start, near, last, own_in, near_in, last_in

    am_spread = spread(lambda ii, h: am.at[h, part_rows(ii), :], ax_s, ax_r, ac_s, ac_r)
    half = NCT // 2
    bt_spread = spread(lambda ii, h: bt.at[pl.ds(h * half, half), part_rows(ii), :], xs_s, xs_r, co_s, co_r)

    def tables():
        for c in (local[6], *local[8:10]):
            c.wait()
        to = dest_v[...]
        mine = used & (owner == p)
        first = jnp.min(jnp.where(mine, slot, 99), axis=0, keepdims=True)
        second = jnp.max(jnp.where(mine, slot, -1), axis=0, keepdims=True)
        place = col_v[...] * 2 + (to & 1) - 48
        key0 = jnp.sum(jnp.where(mine & (slot == first), place, 0), axis=0, keepdims=True) + 48
        key1 = jnp.sum(
            jnp.where(mine & (slot == second) & (second > first), place, 0), axis=0, keepdims=True) + 48
        across = jnp.broadcast_to(jnp.concatenate([key0, key1], axis=1), (128, 128))
        n = iota((128, 128), 0)
        dy = (y + NY - lax.shift_right_logical(n, 4)) & 3
        off = (n + NZ - z) & 15
        turn = jnp.where(off < 8, 2 * off, jnp.where(off == 8, NZ - 1, 31 - 2 * off))
        value = dy * 32 + turn * 2 + lax.shift_right_logical(n, 6)
        rows = list(chain(across.T, across, value))
        own = jnp.sum(
            jnp.where(iota((SLOTS, 64), 1) == p, row_v[...] * NCT + col_v[...], 0),
            axis=1, keepdims=True)
        own = jnp.where(iota((SLOTS, 1), 0) < count_s[0, p], own, 48)
        own = jnp.concatenate([own, jnp.full((128 - SLOTS, 1), 99, I32)], axis=0)
        down = jnp.broadcast_to(own, (128, 128))
        rows += chain(down, down.T, n)
        for n, line in enumerate(rows):
            tab_v[n:n + 1, :] = jnp.clip(line, 0, 127 if n < 4 else SLOTS - 1)
        for d in range(2):
            pick(next_v, 8 * d, lax.rem(z + 1 + (NZ - 2) * d, NZ))
        out = [pltpu.make_async_copy(tab_v, tab_s, loc.at[12]), pltpu.make_async_copy(next_v, next_s, loc.at[13])]
        for c in out:
            c.start()
        return out

    for s in range(steps + BEHIND):
        sw = s - BEHIND
        for h in range(CUTS):
            for d in range(2):
                t_wait(s, d, h)
                t_send(s + 1, d, h)
            for d in range(2 if h < 2 and sw >= 0 else 0):
                z_wait(sw, d, h)
                z_send(sw + 1, d, h)
        if s < steps:
            choose(s + 1)
        if sw >= 0:
            y_forward(sw + 1)
        if s == 0:
            tab_copy = tables()
        if s == 1:
            for c in tab_copy:
                c.wait()
            lax.fori_loop(0, SLOTS, place_slices, jnp.zeros((PART, TILE), F32))
            for r in range(2):
                for c in range(12):
                    ams[r, :, c * TILE:(c + 1) * TILE] = a_place(ams_pre, r, c, ym, yf)
            send(ams, am.at[:, part_rows(i), :], ay_s.at[0], ay_r.at[0], yn[0])
        if s == 2:
            local[10].wait()
            lax.fori_loop(0, SLOTS, place_a, jnp.zeros((TILE, TILE), F32))
        if s == 3:
            arrived(am.at[:, part_rows(i), :], ay_s.at[0], ay_r.at[0], yn[0])
            am_spread[0]()
            for r in range(2):
                for c in range(12):
                    a[r * TILE:(r + 1) * TILE, c * TILE:(c + 1) * TILE] = a_place(a_pre, r, c, y, yr)
        if s == 5:
            am_spread[1]()
        if s == 7:
            am_spread[2]()
        if sw >= LAG:
            y_relay(sw - LAG)

    for g in range(steps + 1):
        for dy in (1, 3, 2):
            arrived(y_piece(yrecv, dy, g), ty_s.at[dy - 1, g], ty_r.at[dy - 1, g], at(y + dy, z))

    def add_up(j, run):
        run = yrecv[tab_s[0, j]].astype(F32) + tab_s[1, j].astype(F32) * run
        pre[j] = run
        return run

    lax.fori_loop(0, 128, add_up, jnp.zeros((PART, TILE), F32), unroll=8)

    for q in range(2 * NCT):
        c, r = q // 2, q % 2
        bt[c, part_rows(i), r * TILE:(r + 1) * TILE] = (pre[tab_s[2, q]] * tab_s[3, q].astype(F32)).astype(BF16)

    bt_spread[0]()
    for g in range(steps - LAG, steps + 1):
        y_relay(g)

    for take in am_spread[3:]:
        take()

    def wl_rows(yy):
        return w[0, pl.ds(pl.multiple_of(yy * DEPTH, DEPTH), DEPTH), :]

    def half_ladder(buf, acc):
        for n, yy in enumerate((y, yr)):
            left = buf[..., n * DEPTH:(n + 1) * DEPTH].reshape(2 * TILE, DEPTH)
            add = jnp.dot(left, wl_rows(yy), preferred_element_type=F32)
            acc[...] = acc[...] + add if n else add

    for g in range(steps + 1):
        for j, zz in group(g):
            arrived(w_at(yr, zz, 0), y1_s.at[2, j], y1_r.at[2, j], yn[1])
    half_ladder(am, acc_p)
    send(acc_p, from_mate, pc_s.at[0], pc_r.at[0], yn[0])
    def cycle(xx, fresh=False):
        xx = lax.rem(xx + NX, NX)
        left = bt[:, pl.ds(pl.multiple_of(xx * 2 * PART, 2 * PART), 2 * PART), :].reshape(DEPTH, 2 * TILE)
        right = jnp.concatenate(
            [w[1, pl.ds(pl.multiple_of(c * TILE + xx * 2 * PART, 2 * PART), 2 * PART), :] for c in range(NCT)], axis=0)
        add = lax.dot_general(left, right, (((0,), (0,)), ((), ())), preferred_element_type=F32)
        acc_c[...] = add if fresh else acc_c[...] + add

    bt_spread[1]()
    for g in range(steps + 1):
        for j, zz in group(g):
            arrived(w_at(yf, zz, 1), y2_s.at[j], y2_r.at[j], yn[int(j in RIM_OUT)])
    bt_spread[3]()
    cycle(x, True)
    half_ladder(a, acc_l)
    bt_spread[2]()
    bt_spread[4]()
    cycle(x + 1)
    cycle(x - 1)
    bt_spread[5]()
    cycle(x + 2)
    out_c[...] = acc_c[...].astype(BF16)
    arrived(from_mate, pc_s.at[0], pc_r.at[0], yn[0])
    out_l[...] = (acc_l[...] + from_mate[...]).astype(BF16)

    for c in sends:
        c.wait_send()


def shards(
    amp_tiles, amp_row, amp_col, amp_dest, amp_count,
    ladder_ints, ladder_present, cycle_ints, cycle_present,
):
    vmem, anywhere = pl.BlockSpec(memory_space=pltpu.VMEM), pl.BlockSpec(memory_space=pl.ANY)
    dma = pltpu.SemaphoreType.DMA
    out = jax.ShapeDtypeStruct((2 * TILE, COLS), BF16)
    return pl.pallas_call(
        kernel,
        out_shape=(out, out),
        in_specs=[anywhere] * 9,
        out_specs=(vmem, vmem),
        scratch_shapes=[
            pltpu.VMEM((2, NCT * TILE, COLS), BF16),
            pltpu.VMEM((96, PART, TILE), BF16),
            pltpu.VMEM((128, PART, TILE), BF16),
            pltpu.VMEM((128, PART, TILE), F32),
            pltpu.VMEM((NCT, TILE, 2 * TILE), BF16),
            pltpu.VMEM((SLOTS, TILE, TILE), BF16),
            pltpu.VMEM((SLOTS, TILE, TILE), F32),
            pltpu.VMEM((2 * TILE, 2 * DEPTH), BF16),
            *[pltpu.VMEM((2 * TILE, COLS), F32)] * 4,
            pltpu.VMEM((2, PART, 2 * DEPTH), BF16),
            pltpu.VMEM((SLOTS, PART, TILE), F32),
            pltpu.VMEM((2, TILE, 2 * DEPTH), BF16),
            pltpu.VMEM((SLOTS, 64), I32), pltpu.VMEM((SLOTS, 64), I32), pltpu.VMEM((SLOTS, 64), I32),
            pltpu.VMEM((1, 64), I32), pltpu.VMEM((2, ROWS, COLS), BF16),
            pltpu.SMEM((3, NCT), I32), pltpu.SMEM((3, NCT), I32), pltpu.SMEM((1, 64), I32),
            pltpu.VMEM((8, 64), I32), pltpu.VMEM((8, TILE), I32),
            pltpu.SMEM((8, 64), I32), pltpu.SMEM((8, TILE), I32),
            pltpu.VMEM((16, 64), I32), pltpu.SMEM((16, 64), I32),
            dma((14,)),
            dma((2, 2 * NZ)), dma((2, 2 * NZ)),
            dma((3, NZ)), dma((3, NZ)), dma((NZ,)), dma((NZ,)),
            dma((NY - 1, 9)), dma((NY - 1, 9)), dma((2, 8 * CUTS)), dma((2, 8 * CUTS)),
            dma((2, 3)), dma((2, 3)), dma((8,)), dma((8,)), dma((2, 3)), dma((2, 3)), dma((8,)), dma((8,)),
            dma((1,)), dma((1,)), dma((1,)), dma((1,)),
            *[pltpu.VMEM((SLOTS, PART, TILE), BF16)] * NZ, *[pltpu.VMEM((8, PART, TILE), BF16)] * 4,
        ],
        compiler_params=pltpu.CompilerParams(
            collective_id=0, has_side_effects=True, vmem_limit_bytes=ROOM * 2**20),
        cost_estimate=pl.CostEstimate(flops=1_300_000_000, bytes_accessed=3_000_000, transcendentals=0),
    )(
        amp_dest.T, amp_col.T, amp_row.T, amp_count.reshape(1, -1), ladder_present.T, cycle_present.T,
        ladder_ints, cycle_ints, amp_tiles,
    )


def solution(mesh):
    placed = (
        P("pair", None, None), P(), P(), P(), P(),
        P("pair", "ints"), P(None, "ints"), P("pair", "ints"), P(None, "ints"),
    )
    return jax.shard_map(
        shards,
        mesh=mesh,
        in_specs=placed,
        out_specs=(P("pair", "ints"), P("pair", "ints")),
        check_vma=False,
    )
```

```python
import jax
import jax.numpy as jnp
from jax import lax
from jax.experimental import pallas as pl
from jax.experimental.pallas import tpu as pltpu
from jax.sharding import PartitionSpec as P

TILE = 128
NCT = 24
SLOTS = 24
NY = 4
NZ = 16
NX = 4
PART = 16
ROWS = 48
COLS = 384
DEPTH = NZ * ROWS
LAG = 5
W_REACH = (8, 7)
T_REACH = (7, 8)
LAST = (NZ - T_REACH[0], T_REACH[1])
CUTS = 2
BEHIND = 0
RIM_OUT = (3, 5, 6, 7, 8, 9, 11, 13)
ROOM = 56
MESH = pl.DeviceIdType.MESH
F32 = jnp.float32
BF16 = jnp.bfloat16
I32 = jnp.int32


def iota(shape, dim):
    return lax.broadcasted_iota(I32, shape, dim)


def chain(down, across, value):
    i, j = iota((128, 128), 0), iota((128, 128), 1)
    tie = down == across
    rank = jnp.sum(jnp.where((across < down) | (tie & (j < i)), 1, 0), axis=1, keepdims=True)
    joined = jnp.max(jnp.where(tie & (j < i), 1, 0), axis=1, keepdims=True)
    here = rank == j
    order = jnp.sum(jnp.where(here, value, 0), axis=0, keepdims=True)
    cont = jnp.sum(jnp.where(here, joined, 0), axis=0, keepdims=True)
    last = jnp.sum(jnp.where(down <= j, 1, 0), axis=0, keepdims=True) - 1
    some = jnp.max(jnp.where(down == j, 1, 0), axis=0, keepdims=True)
    return order, cont, jnp.maximum(last, 0), some


def kernel(
    dest, col, row, count, lp, cp, wl, wr, tiles,
    out_l, out_c,
    w, ysend, yrecv, pre, bt, a_src, a_pre, a, acc_l, acc_c, acc_p, from_mate, ams, ams_pre, am,
    dest_v, col_v, row_v, count_v, w_in, lp_s, cp_s, count_s, sel_v, tab_v, sel_s, tab_s, next_v, next_s,
    loc, zw_s, zw_r, y1_s, y1_r, y2_s, y2_r, ty_s, ty_r, tz_s, tz_r, xs_s, xs_r, co_s, co_r,
    ax_s, ax_r, ac_s, ac_r, ay_s, ay_r, pc_s, pc_r, *t,
):
    p = lax.axis_index("pair")
    i = lax.axis_index("ints")
    y, z = p // NZ, p % NZ
    x, core = i // 2, i % 2

    def at(yy, zz):
        return (lax.rem(yy + NY, NY) * NZ + lax.rem(zz + NZ, NZ), i)

    def at_x(xx):
        return (p, lax.rem(xx + NX, NX) * 2 + core)

    zn = (at(y, z + 1), at(y, z - 1))
    odd = lax.rem(y, 2)
    ym, yr, yf = y + 1 - 2 * odd, lax.rem(y + 3 + 2 * odd, NY), lax.rem(y + 2, NY)
    yn = (at(ym, z), at(yr, z))
    xn = (at_x(x + 1), at_x(x - 1))
    twin = (p, x * 2 + 1 - core)

    pairs = [
        (tiles.at[:, pl.ds(pl.multiple_of(PART * i, PART), PART), :], t[0]),
        (wl, w_in.at[0]), (wr, w_in.at[1]), (lp, lp_s), (cp, cp_s),
        (dest, dest_v), (count, count_s), (count, count_v), (col, col_v), (row, row_v), (tiles, a_src),
    ]
    local = [pltpu.make_async_copy(src, dst, loc.at[n]) for n, (src, dst) in enumerate(pairs)]
    for c in local:
        c.start()

    barrier = pltpu.get_barrier_semaphore()
    greet = [*zn, *xn, twin] + [at(y + d, z) for d in range(1, NY)]
    for dev in greet:
        pl.semaphore_signal(barrier, inc=1, device_id=dev, device_id_type=MESH)

    sends = []

    def send(src, dst, ss, rs, dev):
        c = pltpu.make_async_remote_copy(
            src_ref=src, dst_ref=dst, send_sem=ss, recv_sem=rs, device_id=dev, device_id_type=MESH)
        c.start()
        sends.append(c)

    def arrived(buf, ss, rs, dev):
        pltpu.make_async_remote_copy(
            src_ref=buf, dst_ref=buf, send_sem=ss, recv_sem=rs, device_id=dev, device_id_type=MESH).wait_recv()

    def w_at(yy, zz, part=None):
        q = lax.rem(yy + NY, NY) * NZ + lax.rem(zz + NZ, NZ)
        rows = pl.ds(pl.multiple_of(q * ROWS, PART), ROWS)
        if part is None:
            return w.at[:, rows, :]
        return w.at[part, rows, :]

    def t_send(s, d, h):
        cut = pl.ds(h * (SLOTS // CUTS), SLOTS // CUTS)
        here, there = ((NZ - s) % NZ, NZ - s - 1) if d == 0 else (s, s + 1)
        if s == T_REACH[d] - 1 and h == CUTS - 1:
            zz = lax.rem(z + here, NZ)
            for q in range(8):
                t[18 + d][q] = t[here][next_s[8 * d + q, y * NZ + zz]]
            send(t[18 + d], t[16 + d], tz_s.at[d, s * CUTS], tz_r.at[d, s * CUTS], zn[d])
        elif s < T_REACH[d] - 1:
            src = t[here].at[cut]
            if s == 0:
                src = tiles.at[cut, pl.ds(pl.multiple_of(PART * i, PART), PART), :]
            send(src, t[there].at[cut], tz_s.at[d, s * CUTS + h], tz_r.at[d, s * CUTS + h], zn[d])

    def t_wait(s, d, h):
        if s == T_REACH[d] - 1 and h == CUTS - 1:
            arrived(t[16 + d], tz_s.at[d, s * CUTS], tz_r.at[d, s * CUTS], zn[d])
        elif s < T_REACH[d] - 1:
            cut = pl.ds(h * (SLOTS // CUTS), SLOTS // CUTS)
            arrived(t[NZ - s - 1 if d == 0 else s + 1].at[cut], tz_s.at[d, s * CUTS + h], tz_r.at[d, s * CUTS + h], zn[d])

    pl.semaphore_wait(barrier, len(greet))
    for h in range(CUTS):
        for d in range(2):
            t_send(0, d, h)

    for c in local[1:5]:
        c.wait()
    for k, present in enumerate((lp_s, cp_s)):
        for g in range(ROWS // PART):
            line = (3 * p + g) // 8
            for n in range(COLS // TILE):
                keep = present[n, line].astype(F32)
                block = w_in[k, g * PART:(g + 1) * PART, n * TILE:(n + 1) * TILE].astype(F32)
                w[k, pl.ds(pl.multiple_of(ROWS * p + g * PART, PART), PART), n * TILE:(n + 1) * TILE] = (
                    block * keep).astype(BF16)

    reach = W_REACH
    steps = NZ // 2

    def group(g):
        if g == 0:
            return [(0, z)]
        near = [(NZ - g, z - g)] if g <= reach[0] else []
        return near + ([(g, z + g)] if g <= reach[1] else [])

    def y_forward(g):
        for j, zz in group(g):
            send(w_at(y, zz, 1), w_at(y, zz, 1), y1_s.at[1, j], y1_r.at[1, j], yn[1])
            send(w_at(y, zz, 1), w_at(y, zz, 1), y1_s.at[0, j], y1_r.at[0, j], yn[0])
            send(w_at(y, zz, 0), w_at(y, zz, 0), y1_s.at[2, j], y1_r.at[2, j], yn[1])

    def y_relay(g):
        for j, zz in group(g):
            arrived(w_at(yr, zz, 1), y1_s.at[1, j], y1_r.at[1, j], yn[1])
            arrived(w_at(ym, zz, 1), y1_s.at[0, j], y1_r.at[0, j], yn[0])
            e = int(j in RIM_OUT)
            part = w_at(ym if e else yr, zz, 1)
            send(part, part, y2_s.at[j], y2_r.at[j], yn[e])

    def z_send(s, d, k):
        zz = z - s if d == 0 else z + s
        if s < reach[d]:
            send(w_at(y, zz, k), w_at(y, zz, k), zw_s.at[d, 2 * s + k], zw_r.at[d, 2 * s + k], zn[d])

    def z_wait(s, d, k):
        zz = z - s - 1 if d == 0 else z + s + 1
        if s < reach[d]:
            arrived(w_at(y, zz, k), zw_s.at[d, 2 * s + k], zw_r.at[d, 2 * s + k], zn[d])

    for k in (1, 0):
        for d in range(2):
            z_send(0, d, k)
    y_forward(0)

    for c in local[5:8:2]:
        c.wait()
    slot = iota((SLOTS, 64), 0)
    used = slot < count_v[...]
    owner = lax.shift_right_logical(dest_v[...], 1)

    def pick(table, lo, zz):
        for yy in range(NY):
            hit = used & (owner == yy * NZ + zz)
            first = jnp.min(jnp.where(hit, slot, SLOTS - 1), axis=0, keepdims=True)
            second = jnp.max(jnp.where(hit, slot, 0), axis=0, keepdims=True)
            table[lo + 2 * yy:lo + 2 * yy + 1, :] = jnp.clip(first, 0, SLOTS - 1)
            table[lo + 2 * yy + 1:lo + 2 * yy + 2, :] = jnp.clip(second, 0, SLOTS - 1)

    pick(sel_v, 0, z)
    sel_copy = pltpu.make_async_copy(sel_v, sel_s, loc.at[11])
    sel_copy.start()
    local[0].wait()
    sel_copy.wait()

    def span(g):
        return (0, 1) if g == 0 else (NZ - 1, 1) if g == NZ // 2 else (2 * g - 1, 2)

    def y_piece(buf, dy, g):
        lo, num = span(g)
        return buf.at[pl.ds((dy * NZ + lo) * 2, num * 2)]

    def choose(g):
        far = [g] if g in (0, NZ // 2) else [NZ - g, g]
        for n, zz in enumerate([z + o for o in far]):
            zz = lax.rem(zz + NZ, NZ)
            for dy in (1, 2, 3, 0):
                yy = lax.rem(y + dy, NY)
                for j in range(2):
                    buf, row = (ysend, dy - 1) if dy else (yrecv, 0)
                    if far[n] in LAST:
                        tile = t[16 + LAST.index(far[n])][2 * yy + j]
                    else:
                        tile = t[far[n]][sel_s[2 * yy + j, y * NZ + zz]]
                    buf[(row * NZ + span(g)[0] + n) * 2 + j] = tile
        for dy in (1, 3, 2):
            send(y_piece(ysend, dy - 1, g), y_piece(yrecv, dy, g),
                 ty_s.at[dy - 1, g], ty_r.at[dy - 1, g], at(y + dy, z))

    choose(0)

    def place_a(j, run):
        run = a_src[tab_s[4, j]].astype(F32) + tab_s[5, j].astype(F32) * run
        a_pre[j] = run
        return run

    def place_slices(j, run):
        run = t[0][tab_s[4, j]].astype(F32) + tab_s[5, j].astype(F32) * run
        ams_pre[j] = run
        return run

    def a_place(buf, r, c, first, second):
        q = r * NCT + (first * 6 + c if c < 6 else second * 6 + c - 6)
        return (buf[tab_s[6, q]] * tab_s[7, q].astype(F32)).astype(BF16)

    def part_rows(ii):
        return pl.ds(pl.multiple_of(ii * PART, PART), PART)

    def other(ii):
        return lax.div(ii, 2) * 2 + 1 - lax.rem(ii, 2)

    def spread(piece, xs, xr, cs, cr):
        def start():
            for n in range(2):
                for d in range(2):
                    send(piece(i, (d + n) % 2), piece(i, (d + n) % 2), xs.at[d, n], xr.at[d, n], xn[d])
            for h in range(2):
                send(piece(i, h), piece(i, h), cs.at[h], cr.at[h], twin)

        def near():
            for n in range(2):
                for d in range(2):
                    part = piece(xn[1 - d][1], (d + n) % 2)
                    arrived(part, xs.at[d, n], xr.at[d, n], xn[d])
                    if n == 0:
                        send(part, part, xs.at[d, 2], xr.at[d, 2], xn[d])
                    send(part, part, cs.at[2 + 2 * n + d], cr.at[2 + 2 * n + d], twin)

        def last():
            for d in range(2):
                part = piece(at_x(x + 2)[1], d)
                arrived(part, xs.at[d, 2], xr.at[d, 2], xn[d])
                send(part, part, cs.at[6 + d], cr.at[6 + d], twin)

        def own_in():
            for h in range(2):
                arrived(piece(other(i), h), cs.at[h], cr.at[h], twin)

        def near_in():
            for n in range(2):
                for d in range(2):
                    part = piece(other(xn[1 - d][1]), (d + n) % 2)
                    arrived(part, cs.at[2 + 2 * n + d], cr.at[2 + 2 * n + d], twin)

        def last_in():
            for d in range(2):
                arrived(piece(other(at_x(x + 2)[1]), d), cs.at[6 + d], cr.at[6 + d], twin)

        return start, near, last, own_in, near_in, last_in

    am_spread = spread(lambda ii, h: am.at[h, part_rows(ii), :], ax_s, ax_r, ac_s, ac_r)
    half = NCT // 2
    bt_spread = spread(lambda ii, h: bt.at[pl.ds(h * half, half), part_rows(ii), :], xs_s, xs_r, co_s, co_r)

    def tables():
        for c in (local[6], *local[8:10]):
            c.wait()
        to = dest_v[...]
        mine = used & (owner == p)
        first = jnp.min(jnp.where(mine, slot, 99), axis=0, keepdims=True)
        second = jnp.max(jnp.where(mine, slot, -1), axis=0, keepdims=True)
        place = col_v[...] * 2 + (to & 1) - 48
        key0 = jnp.sum(jnp.where(mine & (slot == first), place, 0), axis=0, keepdims=True) + 48
        key1 = jnp.sum(
            jnp.where(mine & (slot == second) & (second > first), place, 0), axis=0, keepdims=True) + 48
        across = jnp.broadcast_to(jnp.concatenate([key0, key1], axis=1), (128, 128))
        n = iota((128, 128), 0)
        dy = (y + NY - lax.shift_right_logical(n, 4)) & 3
        off = (n + NZ - z) & 15
        turn = jnp.where(off < 8, 2 * off, jnp.where(off == 8, NZ - 1, 31 - 2 * off))
        value = dy * 32 + turn * 2 + lax.shift_right_logical(n, 6)
        rows = list(chain(across.T, across, value))
        own = jnp.sum(
            jnp.where(iota((SLOTS, 64), 1) == p, row_v[...] * NCT + col_v[...], 0),
            axis=1, keepdims=True)
        own = jnp.where(iota((SLOTS, 1), 0) < count_s[0, p], own, 48)
        own = jnp.concatenate([own, jnp.full((128 - SLOTS, 1), 99, I32)], axis=0)
        down = jnp.broadcast_to(own, (128, 128))
        rows += chain(down, down.T, n)
        for n, line in enumerate(rows):
            tab_v[n:n + 1, :] = jnp.clip(line, 0, 127 if n < 4 else SLOTS - 1)
        for d in range(2):
            pick(next_v, 8 * d, lax.rem(z + 1 + (NZ - 2) * d, NZ))
        out = [pltpu.make_async_copy(tab_v, tab_s, loc.at[12]), pltpu.make_async_copy(next_v, next_s, loc.at[13])]
        for c in out:
            c.start()
        return out

    for s in range(steps + BEHIND):
        sw = s - BEHIND
        for h in range(CUTS):
            for d in range(2):
                t_wait(s, d, h)
                t_send(s + 1, d, h)
            if h == 0:
                for d in range(2):
                    z_wait(sw, d, 1)
                    z_send(sw + 1, d, 1)
        if s < steps:
            choose(s + 1)
        for d in range(2):
            z_wait(sw, d, 0)
            z_send(sw + 1, d, 0)
        if sw >= 0:
            y_forward(sw + 1)
        if s == 0:
            tab_copy = tables()
        if s == 1:
            for c in tab_copy:
                c.wait()
            lax.fori_loop(0, SLOTS, place_slices, jnp.zeros((PART, TILE), F32))
            for r in range(2):
                for c in range(12):
                    ams[r, :, c * TILE:(c + 1) * TILE] = a_place(ams_pre, r, c, ym, yf)
            send(ams, am.at[:, part_rows(i), :], ay_s.at[0], ay_r.at[0], yn[0])
        if s == 2:
            local[10].wait()
            lax.fori_loop(0, SLOTS, place_a, jnp.zeros((TILE, TILE), F32))
        if s == 3:
            arrived(am.at[:, part_rows(i), :], ay_s.at[0], ay_r.at[0], yn[0])
            am_spread[0]()
            for r in range(2):
                for c in range(12):
                    a[r * TILE:(r + 1) * TILE, c * TILE:(c + 1) * TILE] = a_place(a_pre, r, c, y, yr)
        if s == 5:
            am_spread[1]()
        if s == 7:
            am_spread[2]()
        if sw >= LAG:
            y_relay(sw - LAG)

    for g in range(steps + 1):
        for dy in (1, 3, 2):
            arrived(y_piece(yrecv, dy, g), ty_s.at[dy - 1, g], ty_r.at[dy - 1, g], at(y + dy, z))

    def add_up(j, run):
        run = yrecv[tab_s[0, j]].astype(F32) + tab_s[1, j].astype(F32) * run
        pre[j] = run
        return run

    lax.fori_loop(0, 128, add_up, jnp.zeros((PART, TILE), F32), unroll=8)

    for q in range(2 * NCT):
        c, r = q // 2, q % 2
        bt[c, part_rows(i), r * TILE:(r + 1) * TILE] = (pre[tab_s[2, q]] * tab_s[3, q].astype(F32)).astype(BF16)

    bt_spread[0]()
    for g in range(steps - LAG, steps + 1):
        y_relay(g)

    for take in am_spread[3:]:
        take()

    def wl_rows(yy):
        return w[0, pl.ds(pl.multiple_of(yy * DEPTH, DEPTH), DEPTH), :]

    def half_ladder(buf, acc):
        for n, yy in enumerate((y, yr)):
            left = buf[..., n * DEPTH:(n + 1) * DEPTH].reshape(2 * TILE, DEPTH)
            add = jnp.dot(left, wl_rows(yy), preferred_element_type=F32)
            acc[...] = acc[...] + add if n else add

    for g in range(steps + 1):
        for j, zz in group(g):
            arrived(w_at(yr, zz, 0), y1_s.at[2, j], y1_r.at[2, j], yn[1])
    half_ladder(am, acc_p)
    send(acc_p, from_mate, pc_s.at[0], pc_r.at[0], yn[0])
    def cycle(xx, fresh=False):
        xx = lax.rem(xx + NX, NX)
        left = bt[:, pl.ds(pl.multiple_of(xx * 2 * PART, 2 * PART), 2 * PART), :].reshape(DEPTH, 2 * TILE)
        right = jnp.concatenate(
            [w[1, pl.ds(pl.multiple_of(c * TILE + xx * 2 * PART, 2 * PART), 2 * PART), :] for c in range(NCT)], axis=0)
        add = lax.dot_general(left, right, (((0,), (0,)), ((), ())), preferred_element_type=F32)
        acc_c[...] = add if fresh else acc_c[...] + add

    bt_spread[1]()
    for g in range(steps + 1):
        for j, zz in group(g):
            arrived(w_at(yf, zz, 1), y2_s.at[j], y2_r.at[j], yn[int(j in RIM_OUT)])
    bt_spread[3]()
    cycle(x, True)
    half_ladder(a, acc_l)
    bt_spread[2]()
    bt_spread[4]()
    cycle(x + 1)
    cycle(x - 1)
    bt_spread[5]()
    cycle(x + 2)
    out_c[...] = acc_c[...].astype(BF16)
    arrived(from_mate, pc_s.at[0], pc_r.at[0], yn[0])
    out_l[...] = (acc_l[...] + from_mate[...]).astype(BF16)

    for c in sends:
        c.wait_send()


def shards(
    amp_tiles, amp_row, amp_col, amp_dest, amp_count,
    ladder_ints, ladder_present, cycle_ints, cycle_present,
):
    vmem, anywhere = pl.BlockSpec(memory_space=pltpu.VMEM), pl.BlockSpec(memory_space=pl.ANY)
    dma = pltpu.SemaphoreType.DMA
    out = jax.ShapeDtypeStruct((2 * TILE, COLS), BF16)
    return pl.pallas_call(
        kernel,
        out_shape=(out, out),
        in_specs=[anywhere] * 9,
        out_specs=(vmem, vmem),
        scratch_shapes=[
            pltpu.VMEM((2, NCT * TILE, COLS), BF16),
            pltpu.VMEM((96, PART, TILE), BF16),
            pltpu.VMEM((128, PART, TILE), BF16),
            pltpu.VMEM((128, PART, TILE), F32),
            pltpu.VMEM((NCT, TILE, 2 * TILE), BF16),
            pltpu.VMEM((SLOTS, TILE, TILE), BF16),
            pltpu.VMEM((SLOTS, TILE, TILE), F32),
            pltpu.VMEM((2 * TILE, 2 * DEPTH), BF16),
            *[pltpu.VMEM((2 * TILE, COLS), F32)] * 4,
            pltpu.VMEM((2, PART, 2 * DEPTH), BF16),
            pltpu.VMEM((SLOTS, PART, TILE), F32),
            pltpu.VMEM((2, TILE, 2 * DEPTH), BF16),
            pltpu.VMEM((SLOTS, 64), I32), pltpu.VMEM((SLOTS, 64), I32), pltpu.VMEM((SLOTS, 64), I32),
            pltpu.VMEM((1, 64), I32), pltpu.VMEM((2, ROWS, COLS), BF16),
            pltpu.SMEM((3, NCT), I32), pltpu.SMEM((3, NCT), I32), pltpu.SMEM((1, 64), I32),
            pltpu.VMEM((8, 64), I32), pltpu.VMEM((8, TILE), I32),
            pltpu.SMEM((8, 64), I32), pltpu.SMEM((8, TILE), I32),
            pltpu.VMEM((16, 64), I32), pltpu.SMEM((16, 64), I32),
            dma((14,)),
            dma((2, 2 * NZ)), dma((2, 2 * NZ)),
            dma((3, NZ)), dma((3, NZ)), dma((NZ,)), dma((NZ,)),
            dma((NY - 1, 9)), dma((NY - 1, 9)), dma((2, 8 * CUTS)), dma((2, 8 * CUTS)),
            dma((2, 3)), dma((2, 3)), dma((8,)), dma((8,)), dma((2, 3)), dma((2, 3)), dma((8,)), dma((8,)),
            dma((1,)), dma((1,)), dma((1,)), dma((1,)),
            *[pltpu.VMEM((SLOTS, PART, TILE), BF16)] * NZ, *[pltpu.VMEM((8, PART, TILE), BF16)] * 4,
        ],
        compiler_params=pltpu.CompilerParams(
            collective_id=0, has_side_effects=True, vmem_limit_bytes=ROOM * 2**20),
        cost_estimate=pl.CostEstimate(flops=1_300_000_000, bytes_accessed=3_000_000, transcendentals=0),
    )(
        amp_dest.T, amp_col.T, amp_row.T, amp_count.reshape(1, -1), ladder_present.T, cycle_present.T,
        ladder_ints, cycle_ints, amp_tiles,
    )


def solution(mesh):
    placed = (
        P("pair", None, None), P(), P(), P(), P(),
        P("pair", "ints"), P(None, "ints"), P("pair", "ints"), P(None, "ints"),
    )
    return jax.shard_map(
        shards,
        mesh=mesh,
        in_specs=placed,
        out_specs=(P("pair", "ints"), P("pair", "ints")),
        check_vma=False,
    )
```
